256 devices in a mesh: dp: 64 (over z, x, core), mp: 4 (over y).
Axes of the slice: x: 4, y: 4, z: 8, core: 2. Of those that a mesh axis runs over, the one named last changes fastest.
Arguments:
- grads: bfloat16 [2, 4096, 8192], P(None, 'dp', 'mp'), may hold values from -6 to 6
- weights: bfloat16 [2, 4096, 8192], P(None, 'dp', 'mp'), may hold values from -6 to 6
- slot_block: int32 [64], replicated, may hold values from 0 to 63, each once
- first_moment: float32 [4, 64, 512, 512], P('mp', 'dp'), may hold values from -100 to 100
- second_moment: float32 [4, 64, 512, 512], P('mp', 'dp'), may hold values from 0.05 to 2
- left_stats: float32 [4, 64, 512, 512], P('mp', 'dp'), as said below
- right_stats: float32 [4, 64, 512, 512], P('mp', 'dp'), as said below
- left_basis: bfloat16 [4, 64, 512, 512], P('mp', 'dp'), as said below
- right_basis: bfloat16 [4, 64, 512, 512], P('mp', 'dp'), as said below
Outputs:
- step_update: bfloat16 [2, 4096, 8192], P(None, 'dp', 'mp')
- first_next: float32 [4, 64, 512, 512], P('mp', 'dp')
- second_next: float32 [4, 64, 512, 512], P('mp', 'dp')
- left_next: float32 [4, 64, 512, 512], P('mp', 'dp')
- right_next: float32 [4, 64, 512, 512], P('mp', 'dp')
- left_basis_next: bfloat16 [4, 64, 512, 512], P('mp', 'dp')
- right_basis_next: bfloat16 [4, 64, 512, 512], P('mp', 'dp')
The draws below stay inside these ranges and needn't reach their ends.
Inputs may be any that keep to these rules, and one draw needn't show every extreme that they name: `slot_block`: each of the 64 block numbers appears once; slot s is kept on the dp device of index s. `left_stats`: symmetric with a dominant positive diagonal. `right_stats`: symmetric with a dominant positive diagonal. `left_basis`: each block is an orthogonal matrix plus a small perturbation. `right_basis`: each block is an orthogonal matrix plus a small perturbation.
All inputs are finite; a program needn't handle non-finite values.
Results may differ from the reference program's by a relative error of at most 0.015.
Values may be sent and summed in bfloat16 or wider, within the bound.
A program may use at most 64 MiB of HBM per device.

```python
import math
import jax
import jax.numpy as jnp
from jax import lax

D = 4096
QW = 8192
BLK = 512
BLKC = 512
MATS = 2
NS_STEPS = 2
MPG = 4
BR = 8
BCL = 4
GBLK = 64
RPB = 8
N_DP = 64


def stats_draw(key, side, spread):
    raw = jax.random.normal(key, (MPG, GBLK, side, side), jnp.float32) * spread
    symmetric = 0.5 * (raw + jnp.swapaxes(raw, -1, -2))
    return symmetric + jnp.eye(side, dtype=jnp.float32) * (2.0 * side)


def draw_left_stats(key, part):
    key = jax.random.fold_in(key, 11)
    return stats_draw(key, BLK, 20.0)


def draw_right_stats(key, part):
    key = jax.random.fold_in(key, 23)
    return stats_draw(key, BLKC, 20.0)


def cosine_block(block_key, side):
    key_rows, key_cols, key_signs = jax.random.split(block_key, 3)
    freq = jax.random.permutation(key_rows, side).astype(jnp.int32)
    place = jax.random.permutation(key_cols, side).astype(jnp.int32)
    signs = (2 * jax.random.randint(key_signs, (side,), 0, 2) - 1).astype(jnp.float32)
    phase = (2 * place[None, :] + 1) * freq[:, None] % (4 * side)
    angle = phase.astype(jnp.float32) * (math.pi / (2.0 * side))
    level = jnp.where(freq == 0, math.sqrt(1.0 / side), math.sqrt(2.0 / side)).astype(jnp.float32)
    return level[:, None] * jnp.cos(angle) * signs[:, None]


def basis_draw(key, side):

    def single(block_key):
        key_base, key_noise = jax.random.split(block_key, 2)
        base = cosine_block(key_base, side)
        noise = jax.random.normal(key_noise, (side, side), jnp.float32) * (0.1 / math.sqrt(side))
        return base + noise
    block_keys = jax.random.split(key, MPG * GBLK)
    whole = jax.vmap(single)(block_keys)
    return whole.reshape(MPG, GBLK, side, side).astype(jnp.bfloat16)


def draw_left_basis(key, part):
    key = jax.random.fold_in(key, 37)

    def single(block_key):
        key_base, key_noise = jax.random.split(block_key, 2)
        sub_keys = jax.random.split(key_base, N_DP)
        subs = jax.vmap(lambda k: cosine_block(k, RPB))(sub_keys)
        eye_small = jnp.eye(N_DP, dtype=jnp.float32)
        base = jnp.einsum('ab,aij->aibj', eye_small, subs).reshape(BLK, BLK)
        noise = jax.random.normal(key_noise, (BLK, BLK), jnp.float32) * (0.1 / math.sqrt(BLK))
        return base + noise
    block_keys = jax.random.split(key, MPG * GBLK)
    whole = jax.vmap(single)(block_keys)
    return whole.reshape(MPG, GBLK, BLK, BLK).astype(jnp.bfloat16)


def draw_right_basis(key, part):
    key = jax.random.fold_in(key, 41)
    return basis_draw(key, BLKC)


def draw_first_moment(key, part):
    key = jax.random.fold_in(key, 53)
    power = 0.5
    raw = jnp.clip(jax.random.normal(key, (MPG, GBLK, BLK, BLKC), jnp.float32), -6.0, 6.0) * 0.5
    rows = jnp.arange(BLK, dtype=jnp.float32) / float(max(BLK - 1, 1))
    slots = jnp.arange(GBLK, dtype=jnp.float32) / float(max(GBLK - 1, 1))
    row_factor = jnp.exp(power * math.log(10.0) * rows)
    slot_factor = jnp.exp(power * math.log(10.0) * slots)
    return raw * row_factor[None, None, :, None] * slot_factor[None, :, None, None]


def shard_levels(stream_key, shape, cuts, low, largest):
    factor_of, own = 1.0, jax.random.fold_in(stream_key, 6)
    for position, blocks in cuts:
        draws = jnp.exp(jax.random.uniform(jax.random.fold_in(own, position), (blocks,), jnp.float32, low / len(cuts), largest / len(cuts)))
        factor_of = factor_of * jnp.repeat(draws, shape[position] // blocks).reshape([-1 if axis == position else 1 for axis in range(len(shape))])
    return factor_of


def centred(own_key, shape, width, limit, cuts=(), kind=jnp.bfloat16):
    values = jax.random.normal(own_key, shape, jnp.float32) * width
    if len(cuts) > 0:
        values = shard_levels(own_key, shape, cuts, -0.22, 0.18) * values
    return jnp.clip(values, min=-limit, max=limit).astype(kind)


def setup_inputs(seed: int = 0) -> dict:
    seeds = jax.random.split(jax.random.key(seed), 10)
    grads = centred(seeds[0], (MATS, D, QW), 1.0, 6.0, ((1, 64), (2, 4)))
    weights = centred(seeds[1], (MATS, D, QW), 1.0, 6.0, ((1, 64), (2, 4)))
    slot_block = jax.random.permutation(seeds[2], GBLK).astype(jnp.int32)
    first_moment = draw_first_moment(jax.random.fold_in(seeds[9], 71), 0)
    second_moment = jnp.clip(jnp.exp(math.log(2.0) - 3.6888794 * jax.random.uniform(seeds[4], (MPG, GBLK, BLK, BLKC), jnp.float32) ** shard_levels(seeds[4], (MPG, GBLK, BLK, BLKC), ((0, 4), (1, 64)), -0.2, 0.2)), 0.05, 2.0)
    left_stats = draw_left_stats(jax.random.fold_in(seeds[9], 71), 0)
    right_stats = draw_right_stats(jax.random.fold_in(seeds[9], 71), 0)
    left_basis = draw_left_basis(jax.random.fold_in(seeds[9], 71), 0)
    right_basis = draw_right_basis(jax.random.fold_in(seeds[9], 71), 0)
    return {"grads": grads, "weights": weights, "slot_block": slot_block, "first_moment": first_moment, "second_moment": second_moment, "left_stats": left_stats, "right_stats": right_stats, "left_basis": left_basis, "right_basis": right_basis}


beta_one = 0.9
beta_two = 0.95
stat_decay = 0.95
adam_eps = 1e-08
clip_rms = 0.2
decay_weight = 0.2
first_fix = 1.0 - 0.9 ** 10
second_fix = 1.0 - 0.95 ** 10
margin = 1.25

def orthogonalize(product):
    norm_value = jnp.sqrt(jnp.sum(product * product) + 1e-12)
    factor = float(product.shape[0]) ** 0.5 / margin
    current = (product * factor / norm_value).astype(jnp.bfloat16)
    for turn in range(NS_STEPS):
        square = jnp.dot(current, current.T, preferred_element_type=jnp.float32).astype(jnp.bfloat16)
        moved = jnp.dot(square, current, preferred_element_type=jnp.float32)
        current = (1.5 * current.astype(jnp.float32) - 0.5 * moved).astype(jnp.bfloat16)
    return current

def update_block(items):
    grad, first, second, left, right, lbasis, rbasis = items
    new_left = stat_decay * left + (1.0 - stat_decay) * jnp.dot(grad, grad.T, preferred_element_type=jnp.float32)
    new_right = stat_decay * right + (1.0 - stat_decay) * jnp.dot(grad.T, grad, preferred_element_type=jnp.float32)
    half = jnp.dot(lbasis.T, grad, preferred_element_type=jnp.float32).astype(jnp.bfloat16)
    rotated = jnp.dot(half, rbasis, preferred_element_type=jnp.float32)
    new_first = beta_one * first + (1.0 - beta_one) * rotated
    new_second = beta_two * second + (1.0 - beta_two) * rotated * rotated
    normalized = (new_first / first_fix / (jnp.sqrt(new_second / second_fix) + adam_eps)).astype(jnp.bfloat16)
    back = jnp.dot(lbasis, normalized, preferred_element_type=jnp.float32).astype(jnp.bfloat16)
    update = jnp.dot(back, rbasis.T, preferred_element_type=jnp.float32).astype(jnp.bfloat16)
    left_new = orthogonalize(jnp.dot(new_left.astype(jnp.bfloat16), lbasis, preferred_element_type=jnp.float32))
    right_new = orthogonalize(jnp.dot(new_right.astype(jnp.bfloat16), rbasis, preferred_element_type=jnp.float32))
    return (new_first, new_second, new_left, new_right, left_new, right_new, update)

def reference(grads, weights, slot_block, first_moment, second_moment, left_stats, right_stats, left_basis, right_basis):
    matrix = grads.reshape(MATS, N_DP, BR, RPB, QW).transpose(0, 2, 1, 3, 4)
    matrix = matrix.reshape(MATS, BR, BLK, MPG, BCL, BLKC)
    blocks = matrix.transpose(3, 0, 1, 4, 2, 5).reshape(MPG, GBLK, BLK, BLKC)
    blocks = jnp.take(blocks, slot_block, axis=1)

    def flat(array):
        return array.reshape((MPG * GBLK,) + array.shape[2:])
    results = lax.map(update_block, (flat(blocks), flat(first_moment), flat(second_moment), flat(left_stats), flat(right_stats), flat(left_basis), flat(right_basis)))
    shaped = [r.reshape((MPG, GBLK) + r.shape[1:]) for r in results]
    updates = shaped[6]
    upd_f = updates.astype(jnp.float32)
    total = jnp.sum(upd_f * upd_f)
    scale = jnp.minimum(1.0, clip_rms / jnp.sqrt(total / float(MATS * D * QW) + 1e-12))
    ordered = jnp.zeros_like(updates).at[:, slot_block].set(updates)
    restored = ordered.reshape(MPG, MATS, BR, BCL, BLK, BLKC).transpose(1, 2, 4, 0, 3, 5)
    restored = restored.reshape(MATS, BR, N_DP, RPB, QW).transpose(0, 2, 1, 3, 4).reshape(MATS, D, QW)
    step_update = (scale * restored.astype(jnp.float32) + decay_weight * weights.astype(jnp.float32)).astype(jnp.bfloat16)
    return (step_update, shaped[0], shaped[1], shaped[2], shaped[3], shaped[4], shaped[5])
```

```python
import functools

import jax
import jax.numpy as jnp
from jax import lax
from jax.experimental import pallas as pl
from jax.experimental.pallas import tpu as pltpu
from jax.sharding import PartitionSpec as P

D = 4096
QW = 8192
MATS = 2
NS_STEPS = 2
beta_one = 0.9
beta_two = 0.95
stat_decay = 0.95
adam_eps = 1e-08
clip_rms = 0.2
decay_weight = 0.2
first_fix = 1.0 - 0.9**10
second_fix = 1.0 - 0.95**10
margin = 1.25

MESH = pl.DeviceIdType.MESH
F32 = jnp.float32
BF16 = jnp.bfloat16
SLAB = 8


def mm(a, b):
    return jnp.dot(a, b, preferred_element_type=F32)


def mm_t(a, b):
    return lax.dot_general(a, b, (((1,), (1,)), ((), ())), preferred_element_type=F32)


def orthogonalize(products):
    currents = []
    for product in products:
        norm_value = jnp.sqrt(jnp.sum(product * product) + 1e-12)
        factor = float(product.shape[0]) ** 0.5 / margin
        currents.append((product * (factor / norm_value)).astype(BF16))
    for turn in range(NS_STEPS):
        squares = [mm_t(x, x).astype(BF16) for x in currents]
        moved = [mm(s, x) for s, x in zip(squares, currents)]
        currents = [
            (1.5 * x.astype(F32) - 0.5 * m).astype(BF16) for x, m in zip(currents, moved)
        ]
    return currents


def kernel(
    n,
    groups,
    dims,
    slot,
    grads_hbm,
    weights_hbm,
    first_hbm,
    second_hbm,
    left_hbm,
    right_hbm,
    lbasis_hbm,
    rbasis_hbm,
    step_out,
    first_out,
    second_out,
    left_out,
    right_out,
    lnext_out,
    rnext_out,
    grads,
    weights,
    first,
    second,
    left,
    right,
    lbasis,
    rbasis,
    onehot,
    onehot_t,
    lbasis_t,
    lrolled,
    normal,
    gsend,
    gbuf,
    usend,
    ubuf,
    parts,
    totals,
    load_sem,
    gsend_sem,
    grecv_sem,
    usend_sem,
    urecv_sem,
    psend_sem,
    precv_sem,
    tsend_sem,
    trecv_sem,
):
    mats, block_rows, block_cols, width = dims
    side = n * SLAB
    stripe = mats * block_rows * SLAB
    me = lax.axis_index("dp")
    mine = lax.axis_index("mp")

    pairs = [
        (grads_hbm, grads),
        (lbasis_hbm, lbasis),
        (rbasis_hbm, rbasis),
        (first_hbm, first),
        (second_hbm, second),
        (left_hbm, left),
        (right_hbm, right),
        (weights_hbm, weights),
    ]
    loads = [pltpu.make_async_copy(a, b, load_sem.at[i]) for i, (a, b) in enumerate(pairs)]
    for load in loads:
        load.start()

    barrier = pltpu.get_barrier_semaphore()

    def greet(k, carry):
        pl.semaphore_signal(
            barrier, inc=1, device_id=(lax.rem(me + k, n), mine), device_id_type=MESH
        )
        return carry

    lax.fori_loop(1, n, greet, 0)
    for k in range(1, groups):
        pl.semaphore_signal(
            barrier, inc=1, device_id=(me, lax.rem(mine + k, groups)), device_id_type=MESH
        )

    columns = lax.broadcasted_iota(jnp.int32, (SLAB, n * SLAB), 1)
    rows = lax.broadcasted_iota(jnp.int32, (SLAB, n * SLAB), 0)

    def pick(s, carry):
        block = slot[s]
        c = lax.rem(block, block_cols)
        rest = block // block_cols
        base = c * stripe + rest * SLAB
        onehot[s] = (columns - rows == base).astype(F32)
        return carry

    lax.fori_loop(0, n, pick, 0)

    loads[0].wait()
    chosen = onehot[...].reshape(side, side).astype(BF16)
    picked = mm(chosen[:, :stripe], grads[:, :width])
    for c in range(1, block_cols):
        picked += mm(
            chosen[:, c * stripe : (c + 1) * stripe], grads[:, c * width : (c + 1) * width]
        )
    gsend[...] = picked.reshape(n, SLAB, width).astype(BF16)

    pl.semaphore_wait(barrier, n - 1 + groups - 1)

    def send_grad(k, carry):
        peer = lax.rem(me + k, n)
        pltpu.make_async_remote_copy(
            src_ref=gsend.at[peer],
            dst_ref=gbuf.at[me],
            send_sem=gsend_sem,
            recv_sem=grecv_sem,
            device_id=(peer, mine),
            device_id_type=MESH,
        ).start()
        return carry

    lax.fori_loop(1, n, send_grad, 0)
    gbuf[me] = gsend[me]

    onehot_t[...] = onehot[...].reshape(side, side).T.astype(BF16)
    loads[1].wait()
    lbasis_t[...] = lbasis[...].T
    ltall = lbasis[...].astype(F32).reshape(n, SLAB, side)
    onehot_l = onehot
    onehot_l[...] = ltall

    def roll(k, carry):
        lrolled[k] = onehot_l[lax.rem(me + k, n)]
        return carry

    lax.fori_loop(0, n, roll, 0)
    for load in loads[2:5]:
        load.wait()

    pltpu.make_async_copy(gbuf.at[pl.ds(0, n - 1)], gbuf.at[pl.ds(0, n - 1)], grecv_sem).wait()
    grad = gbuf[...].astype(F32).reshape(side, width).astype(BF16)
    half = mm(lbasis_t[...], grad).astype(BF16)
    chunks = 4 if side >= 256 else 1
    size = side // chunks
    for c in range(chunks):
        at = slice(c * size, (c + 1) * size)
        rotated = mm(half[at], rbasis[...])
        new_first = beta_one * first[at] + (1.0 - beta_one) * rotated
        new_second = beta_two * second[at] + (1.0 - beta_two) * rotated * rotated
        first_out[at] = new_first
        second_out[at] = new_second
        normal[at] = (
            new_first / first_fix / (jnp.sqrt(new_second / second_fix) + adam_eps)
        ).astype(BF16)

    part = jnp.zeros((1, width), F32)
    for c in range(chunks):
        per = n // chunks
        turned = lrolled[c * per : (c + 1) * per].reshape(size, side).astype(BF16)
        back = mm(turned, normal[...]).astype(BF16)
        update = mm_t(back, rbasis[...]).astype(BF16)
        wide = update.astype(F32)
        usend[c * per : (c + 1) * per] = wide.reshape(per, SLAB, width).astype(BF16)
        part += jnp.sum(wide * wide, axis=0, keepdims=True)

        def send_update(k, carry):
            peer = lax.rem(me + k, n)
            pltpu.make_async_remote_copy(
                src_ref=usend.at[k],
                dst_ref=ubuf.at[me],
                send_sem=usend_sem,
                recv_sem=urecv_sem,
                device_id=(peer, mine),
                device_id_type=MESH,
            ).start()
            return carry

        lax.fori_loop(max(c * per, 1), (c + 1) * per, send_update, 0)
    ubuf[me] = usend[0]

    lanes = sum(part[:, i * 128 : (i + 1) * 128] for i in range(width // 128))
    parts[mine] = lanes
    for k in range(1, groups):
        pltpu.make_async_remote_copy(
            src_ref=parts.at[mine],
            dst_ref=parts.at[mine],
            send_sem=psend_sem,
            recv_sem=precv_sem,
            device_id=(me, lax.rem(mine + k, groups)),
            device_id_type=MESH,
        ).start()

    loads[5].wait()
    loads[6].wait()
    new_left = stat_decay * left[...] + (1.0 - stat_decay) * mm_t(grad, grad)
    left_out[...] = new_left
    new_right = stat_decay * right[...] + (1.0 - stat_decay) * mm(grad.T, grad)
    right_out[...] = new_right

    pltpu.make_async_copy(
        parts.at[pl.ds(0, groups - 1)], parts.at[pl.ds(0, groups - 1)], precv_sem
    ).wait()
    totals[me] = jnp.sum(parts[...], axis=0)

    def send_total(k, carry):
        pltpu.make_async_remote_copy(
            src_ref=totals.at[me],
            dst_ref=totals.at[me],
            send_sem=tsend_sem,
            recv_sem=trecv_sem,
            device_id=(lax.rem(me + k, n), mine),
            device_id_type=MESH,
        ).start()
        return carry

    lax.fori_loop(1, n, send_total, 0)

    left_new, right_new = orthogonalize(
        [mm(left_out[...].astype(BF16), lbasis[...]), mm(right_out[...].astype(BF16), rbasis[...])]
    )
    lnext_out[...] = left_new
    rnext_out[...] = right_new

    loads[7].wait()
    pltpu.make_async_copy(totals.at[pl.ds(0, n - 1)], totals.at[pl.ds(0, n - 1)], trecv_sem).wait()
    total = jnp.sum(totals[...])
    scale = jnp.minimum(1.0, clip_rms / jnp.sqrt(total / float(MATS * D * QW) + 1e-12))
    pltpu.make_async_copy(ubuf.at[pl.ds(0, n - 1)], ubuf.at[pl.ds(0, n - 1)], urecv_sem).wait()
    returned = ubuf[...].astype(F32).reshape(side, width).astype(BF16)
    for c in range(block_cols):
        placed = mm(onehot_t[c * stripe : (c + 1) * stripe, :], returned)
        at = slice(c * width, (c + 1) * width)
        step_out[:, at] = (scale * placed + decay_weight * weights[:, at].astype(F32)).astype(BF16)

    pltpu.make_async_copy(gsend.at[pl.ds(0, n - 1)], gsend.at[pl.ds(0, n - 1)], gsend_sem).wait()
    pltpu.make_async_copy(usend.at[pl.ds(0, n - 1)], usend.at[pl.ds(0, n - 1)], usend_sem).wait()
    pltpu.make_async_copy(
        parts.at[pl.ds(0, groups - 1)], parts.at[pl.ds(0, groups - 1)], psend_sem
    ).wait()
    pltpu.make_async_copy(totals.at[pl.ds(0, n - 1)], totals.at[pl.ds(0, n - 1)], tsend_sem).wait()


def body(n, groups, grads, weights, slot_block, first, second, left, right, lbasis, rbasis):
    mats, rows, cols = grads.shape
    side, width = first.shape[-2:]
    block_rows = rows // SLAB
    block_cols = cols // width
    vmem = pltpu.VMEM
    dma = pltpu.SemaphoreType.DMA
    flat = (mats * rows, cols)
    outs = [
        (flat, BF16),
        ((side, width), F32),
        ((side, width), F32),
        ((side, side), F32),
        ((width, width), F32),
        ((side, side), BF16),
        ((width, width), BF16),
    ]
    results = pl.pallas_call(
        functools.partial(kernel, n, groups, (mats, block_rows, block_cols, width)),
        out_shape=[OUT(shape, kind) for shape, kind in outs],
        in_specs=[pl.BlockSpec(memory_space=pltpu.SMEM)]
        + [pl.BlockSpec(memory_space=pl.ANY)] * 8,
        out_specs=[pl.BlockSpec(memory_space=pltpu.VMEM)] * 7,
        scratch_shapes=[
            vmem(flat, BF16),
            vmem(flat, BF16),
            vmem((side, width), F32),
            vmem((side, width), F32),
            vmem((side, side), F32),
            vmem((width, width), F32),
            vmem((side, side), BF16),
            vmem((width, width), BF16),
            vmem((n, SLAB, n * SLAB), F32),
            vmem((side, side), BF16),
            vmem((side, side), BF16),
            vmem((n, SLAB, side), F32),
            vmem((side, width), BF16),
            vmem((n, SLAB, width), BF16),
            vmem((n, SLAB, width), BF16),
            vmem((n, SLAB, width), BF16),
            vmem((n, SLAB, width), BF16),
            vmem((groups, 1, 128), F32),
            vmem((n, 1, 128), F32),
            dma((8,)),
            dma,
            dma,
            dma,
            dma,
            dma,
            dma,
            dma,
            dma,
        ],
        compiler_params=pltpu.CompilerParams(
            collective_id=0, has_side_effects=True, vmem_limit_bytes=40 * 1024 * 1024
        ),
    )(
        slot_block,
        grads.reshape(flat),
        weights.reshape(flat),
        first[0, 0],
        second[0, 0],
        left[0, 0],
        right[0, 0],
        lbasis[0, 0],
        rbasis[0, 0],
    )
    return (results[0].reshape(grads.shape), *[r[None, None] for r in results[1:]])


OUT = jax.ShapeDtypeStruct


def solution(mesh):
    owned = P("mp", "dp", None, None)
    rows = P(None, "dp", "mp")
    return jax.shard_map(
        functools.partial(body, mesh.shape["dp"], mesh.shape["mp"]),
        mesh=mesh,
        in_specs=(rows, rows, P()) + (owned,) * 6,
        out_specs=(rows,) + (owned,) * 6,
        check_vma=False,
    )
```

```python
import functools

import jax
import jax.numpy as jnp
from jax import lax
from jax.experimental import pallas as pl
from jax.experimental.pallas import tpu as pltpu
from jax.sharding import PartitionSpec as P

D = 4096
QW = 8192
MATS = 2
NS_STEPS = 2
beta_one = 0.9
beta_two = 0.95
stat_decay = 0.95
adam_eps = 1e-08
clip_rms = 0.2
decay_weight = 0.2
first_fix = 1.0 - 0.9**10
second_fix = 1.0 - 0.95**10
margin = 1.25

MESH = pl.DeviceIdType.MESH
F32 = jnp.float32
BF16 = jnp.bfloat16
SLAB = 8


def mm(a, b):
    return jnp.dot(a, b, preferred_element_type=F32)


def mm_t(a, b):
    return lax.dot_general(a, b, (((1,), (1,)), ((), ())), preferred_element_type=F32)


def orthogonalize(products):
    currents = []
    for product in products:
        norm_value = jnp.sqrt(jnp.sum(product * product) + 1e-12)
        factor = float(product.shape[0]) ** 0.5 / margin
        currents.append((product * (factor / norm_value)).astype(BF16))
    for turn in range(NS_STEPS):
        squares = [mm_t(x, x).astype(BF16) for x in currents]
        moved = [mm(s, x) for s, x in zip(squares, currents)]
        currents = [
            (1.5 * x.astype(F32) - 0.5 * m).astype(BF16) for x, m in zip(currents, moved)
        ]
    return currents


def peer_of(k, me, n):
    xs = 4 if n >= 8 else 1
    zs = n // (2 * xs)
    core = lax.div(k, n // 2)
    rest = lax.rem(k, n // 2)
    turn = lax.rem(rest, zs)
    dz = zs // 2 + lax.div(turn + 1, 2) * (1 - 2 * lax.rem(turn, 2))
    dx = lax.div(rest, zs)
    z = lax.rem(lax.div(me, 2 * xs) + dz, zs)
    x = lax.rem(lax.rem(lax.div(me, 2), xs) + dx, xs)
    return (z * xs + x) * 2 + core


def all_of(ref, count, sem):
    part = ref.at[pl.ds(0, count)]
    return pltpu.make_async_copy(part, part, sem)


def exchange_kernel(
    n,
    groups,
    dims,
    slot_hbm,
    grads_hbm,
    weights_hbm,
    first_hbm,
    second_hbm,
    left_hbm,
    right_hbm,
    lbasis_hbm,
    rbasis_hbm,
    first_out,
    second_out,
    left_out,
    right_out,
    lnext_out,
    rnext_out,
    ubuf,
    onehot_t,
    weights,
    totals,
    slot,
    grads,
    first,
    second,
    left,
    right,
    lbasis,
    rbasis,
    onehot,
    lbasis_t,
    lrolled,
    gsend,
    gbuf,
    usend,
    parts,
    load_sem,
    grad_sem,
    gsend_sem,
    grecv_sem,
    usend_sem,
    urecv_sem,
    psend_sem,
    precv_sem,
    tsend_sem,
    trecv_sem,
):
    mats, block_rows, block_cols, width = dims
    side = n * SLAB
    stripe = mats * block_rows * SLAB
    me = lax.axis_index("dp")
    mine = lax.axis_index("mp")

    pairs = [
        (slot_hbm, slot),
        (lbasis_hbm, lbasis),
        (rbasis_hbm, rbasis),
        (first_hbm, first),
        (second_hbm, second),
        (left_hbm, left),
        (right_hbm, right),
        (weights_hbm, weights),
    ]
    loads = [pltpu.make_async_copy(a, b, load_sem.at[i]) for i, (a, b) in enumerate(pairs)]
    per_col = mats * block_rows
    grad_loads = [
        pltpu.make_async_copy(
            grads_hbm.at[:, :, pl.ds(c * width, width)],
            grads.at[pl.ds(c * per_col, per_col)],
            grad_sem.at[c],
        )
        for c in range(block_cols)
    ]
    loads[0].start()
    for load in grad_loads:
        load.start()

    barrier = pltpu.get_barrier_semaphore()

    def greet(k, carry):
        pl.semaphore_signal(
            barrier, inc=1, device_id=(lax.rem(me + k, n), mine), device_id_type=MESH
        )
        return carry

    lax.fori_loop(1, n, greet, 0)
    for k in range(1, groups):
        pl.semaphore_signal(
            barrier, inc=1, device_id=(me, lax.rem(mine + k, groups)), device_id_type=MESH
        )

    loads[0].wait()
    for load in grad_loads:
        load.wait()
    for load in loads[1:]:
        load.start()

    def stage(s, carry):
        block = slot[s]
        c = lax.rem(block, block_cols)
        rest = lax.div(block, block_cols)
        gsend[s] = grads[c * per_col + rest]
        return carry

    lax.fori_loop(0, n, stage, 0, unroll=4)

    pl.semaphore_wait(barrier, n - 1 + groups - 1)

    def send_grad(k, carry):
        peer = peer_of(k, me, n)

        @pl.when(peer != me)
        def _():
            pltpu.make_async_remote_copy(
                src_ref=gsend.at[peer],
                dst_ref=gbuf.at[me],
                send_sem=gsend_sem,
                recv_sem=grecv_sem,
                device_id=(peer, mine),
                device_id_type=MESH,
            ).start()

        return carry

    lax.fori_loop(0, n, send_grad, 0)
    gbuf[me] = gsend[me]

    columns = lax.broadcasted_iota(jnp.int32, (SLAB, side), 1)
    rows = lax.broadcasted_iota(jnp.int32, (SLAB, side), 0)

    def pick(s, carry):
        block = slot[s]
        c = lax.rem(block, block_cols)
        rest = lax.div(block, block_cols)
        base = c * stripe + rest * SLAB
        onehot[s] = (columns - rows == base).astype(F32)
        return carry

    lax.fori_loop(0, n, pick, 0)
    onehot_t[...] = onehot[...].reshape(side, side).T.astype(BF16)
    loads[1].wait()
    lbasis_t[...] = lbasis[...].reshape(side, side).T

    def roll(k, carry):
        lrolled[k] = lbasis[peer_of(k, me, n)]
        return carry

    lax.fori_loop(0, n, roll, 0)
    for load in loads[2:5]:
        load.wait()

    all_of(gbuf, n - 1, grecv_sem).wait()
    grad = gbuf[...].reshape(side, width)
    half = mm(lbasis_t[...], grad).astype(BF16)
    rotated = mm(half, rbasis[...])
    new_first = beta_one * first[...] + (1.0 - beta_one) * rotated
    new_second = beta_two * second[...] + (1.0 - beta_two) * rotated * rotated
    first_out[...] = new_first
    second_out[...] = new_second
    normal = (new_first / first_fix / (jnp.sqrt(new_second / second_fix) + adam_eps)).astype(BF16)
    back = mm(lrolled[...].reshape(side, side), normal).astype(BF16)

    def send_update(k, carry):
        peer = peer_of(k, me, n)

        @pl.when(peer != me)
        def _():
            pltpu.make_async_remote_copy(
                src_ref=usend.at[k],
                dst_ref=ubuf.at[me],
                send_sem=usend_sem,
                recv_sem=urecv_sem,
                device_id=(peer, mine),
                device_id_type=MESH,
            ).start()

        @pl.when(peer == me)
        def _():
            ubuf[me] = usend[k]

        return carry

    part = jnp.zeros((1, width), F32)
    chunks = 2
    size, per = side // chunks, n // chunks
    for c in range(chunks):
        update = mm_t(back[c * size : (c + 1) * size], rbasis[...]).astype(BF16)
        usend[c * per : (c + 1) * per] = update.reshape(per, SLAB, width)
        wide = update.astype(F32)
        part += jnp.sum(wide * wide, axis=0, keepdims=True)
        if c == chunks - 1:
            parts[mine] = sum(part[:, i * 128 : (i + 1) * 128] for i in range(width // 128))
            for k in range(1, groups):
                pltpu.make_async_remote_copy(
                    src_ref=parts.at[mine],
                    dst_ref=parts.at[mine],
                    send_sem=psend_sem,
                    recv_sem=precv_sem,
                    device_id=(me, lax.rem(mine + k, groups)),
                    device_id_type=MESH,
                ).start()
        lax.fori_loop(c * per, (c + 1) * per, send_update, 0)

    loads[5].wait()
    loads[6].wait()
    new_left = stat_decay * left[...] + (1.0 - stat_decay) * mm_t(grad, grad)
    left_out[...] = new_left
    new_right = stat_decay * right[...] + (1.0 - stat_decay) * mm(grad.T, grad)
    right_out[...] = new_right

    all_of(parts, groups - 1, precv_sem).wait()
    totals[me] = jnp.sum(parts[...], axis=0)

    def send_total(k, carry):
        peer = peer_of(k, me, n)

        @pl.when(peer != me)
        def _():
            pltpu.make_async_remote_copy(
                src_ref=totals.at[me],
                dst_ref=totals.at[me],
                send_sem=tsend_sem,
                recv_sem=trecv_sem,
                device_id=(peer, mine),
                device_id_type=MESH,
            ).start()

        return carry

    lax.fori_loop(0, n, send_total, 0)

    left_new, right_new = orthogonalize(
        [
            mm(left_out[...].astype(BF16), lbasis[...].reshape(side, side)),
            mm(right_out[...].astype(BF16), rbasis[...]),
        ]
    )
    lnext_out[...] = left_new
    rnext_out[...] = right_new

    loads[7].wait()
    all_of(gsend, n - 1, gsend_sem).wait()
    all_of(usend, n - 1, usend_sem).wait()
    all_of(parts, groups - 1, psend_sem).wait()
    all_of(totals, n - 1, tsend_sem).wait()
    all_of(totals, n - 1, trecv_sem).wait()
    all_of(ubuf, n - 1, urecv_sem).wait()


def store_kernel(dims, *refs):
    mats, block_rows, block_cols, width = dims
    stripe = mats * block_rows * SLAB
    done, (ubuf, onehot_t, weights, totals), rest = refs[:6], refs[6:10], refs[10:]
    step_hbm, outs, (step, sems) = rest[0], rest[1:7], rest[7:]
    copies = [pltpu.make_async_copy(a, b, sems.at[i]) for i, (a, b) in enumerate(zip(done, outs))]
    for copy in copies:
        copy.start()
    n = ubuf.shape[0]
    total = jnp.sum(totals[...])
    scale = jnp.minimum(1.0, clip_rms / jnp.sqrt(total / float(MATS * D * QW) + 1e-12))
    returned = ubuf[...].reshape(n * SLAB, width)
    for c in range(block_cols):
        placed = mm(onehot_t[c * stripe : (c + 1) * stripe, :], returned)
        at = slice(c * width, (c + 1) * width)
        step[:, at] = (scale * placed + decay_weight * weights[:, at].astype(F32)).astype(BF16)
    last = pltpu.make_async_copy(step, step_hbm, sems.at[6])
    last.start()
    for copy in copies:
        copy.wait()
    last.wait()


def body(n, groups, grads, weights, slot_block, first, second, left, right, lbasis, rbasis):
    mats, rows, cols = grads.shape
    side, width = first.shape[-2:]
    block_rows = rows // SLAB
    block_cols = cols // width
    dims = (mats, block_rows, block_cols, width)
    vmem = pltpu.VMEM
    dma = pltpu.SemaphoreType.DMA
    flat = (mats * rows, cols)
    shape = jax.ShapeDtypeStruct
    owned = [
        shape((side, width), F32),
        shape((side, width), F32),
        shape((side, side), F32),
        shape((width, width), F32),
        shape((side, side), BF16),
        shape((width, width), BF16),
    ]
    passed = [
        shape((n, SLAB, width), BF16),
        shape((side, side), BF16),
        shape(flat, BF16),
        shape((n, 1, 128), F32),
    ]
    here = pl.BlockSpec(memory_space=pltpu.VMEM)
    away = pl.BlockSpec(memory_space=pltpu.HBM)
    results = pl.pallas_call(
        functools.partial(exchange_kernel, n, groups, dims),
        out_shape=owned + passed,
        in_specs=[away] * 9,
        out_specs=[here] * 10,
        scratch_shapes=[
            pltpu.SMEM((n,), jnp.int32),
            vmem((n, SLAB, width), BF16),
            vmem((side, width), F32),
            vmem((side, width), F32),
            vmem((side, side), F32),
            vmem((width, width), F32),
            vmem((n, SLAB, side), BF16),
            vmem((width, width), BF16),
            vmem((n, SLAB, side), F32),
            vmem((side, side), BF16),
            vmem((n, SLAB, side), BF16),
            vmem((n, SLAB, width), BF16),
            vmem((n, SLAB, width), BF16),
            vmem((n, SLAB, width), BF16),
            vmem((groups, 1, 128), F32),
            dma((8,)),
            dma((block_cols,)),
            dma,
            dma,
            dma,
            dma,
            dma,
            dma,
            dma,
            dma,
        ],
        compiler_params=pltpu.CompilerParams(
            collective_id=0, has_side_effects=True, vmem_limit_bytes=40 * 1024 * 1024
        ),
    )(
        *[
            pltpu.with_memory_space_constraint(x, pltpu.HBM)
            for x in (
                slot_block,
                grads.reshape(mats * block_rows, SLAB, cols),
                weights.reshape(flat),
                first[0, 0],
                second[0, 0],
                left[0, 0],
                right[0, 0],
                lbasis[0, 0].reshape(n, SLAB, side),
                rbasis[0, 0],
            )
        ]
    )
    stored = pl.pallas_call(
        functools.partial(store_kernel, dims),
        out_shape=[shape(flat, BF16)] + owned,
        in_specs=[here] * 10,
        out_specs=[away] * 7,
        scratch_shapes=[vmem(flat, BF16), dma((7,))],
        compiler_params=pltpu.CompilerParams(vmem_limit_bytes=40 * 1024 * 1024),
    )(*results)
    return (stored[0].reshape(grads.shape), *[r[None, None] for r in stored[1:]])


def solution(mesh):
    owned = P("mp", "dp", None, None)
    rows = P(None, "dp", "mp")
    return jax.shard_map(
        functools.partial(body, mesh.shape["dp"], mesh.shape["mp"]),
        mesh=mesh,
        in_specs=(rows, rows, P()) + (owned,) * 6,
        out_specs=(rows,) + (owned,) * 6,
        check_vma=False,
    )
```

```python
import functools

import jax
import jax.numpy as jnp
from jax import lax
from jax.experimental import pallas as pl
from jax.experimental.pallas import tpu as pltpu
from jax.sharding import PartitionSpec as P

D = 4096
QW = 8192
MATS = 2
NS_STEPS = 2
beta_one = 0.9
beta_two = 0.95
stat_decay = 0.95
adam_eps = 1e-08
clip_rms = 0.2
decay_weight = 0.2
first_fix = 1.0 - 0.9**10
second_fix = 1.0 - 0.95**10
margin = 1.25

MESH = pl.DeviceIdType.MESH
F32 = jnp.float32
BF16 = jnp.bfloat16
SLAB = 8


def mm(a, b):
    return jnp.dot(a, b, preferred_element_type=F32)


def mm_t(a, b):
    return lax.dot_general(a, b, (((1,), (1,)), ((), ())), preferred_element_type=F32)


def orthogonalize(products):
    currents = []
    for product in products:
        norm_value = jnp.sqrt(jnp.sum(product * product) + 1e-12)
        factor = float(product.shape[0]) ** 0.5 / margin
        currents.append((product * (factor / norm_value)).astype(BF16))
    for turn in range(NS_STEPS):
        squares = [mm_t(x, x).astype(BF16) for x in currents]
        moved = [mm(s, x) for s, x in zip(squares, currents)]
        currents = [
            (1.5 * x.astype(F32) - 0.5 * m).astype(BF16) for x, m in zip(currents, moved)
        ]
    return currents


def far_first(zs):
    return sorted(range(zs), key=lambda j: (abs(2 * j - zs), j))


def all_of(ref, count, sem):
    part = ref.at[pl.ds(0, count)]
    return pltpu.make_async_copy(part, part, sem)


def exchange_kernel(
    n,
    groups,
    dims,
    slot_hbm,
    grads_hbm,
    weights_hbm,
    first_hbm,
    second_hbm,
    left_hbm,
    right_hbm,
    lbasis_hbm,
    rbasis_hbm,
    first_out,
    second_out,
    left_out,
    right_out,
    lnext_out,
    rnext_out,
    ubuf,
    onehot_t,
    weights,
    totals,
    slot,
    grads,
    first,
    second,
    left,
    right,
    lbasis,
    rbasis,
    onehot,
    lbasis_t,
    gsend,
    gbuf,
    usend,
    parts,
    load_sem,
    grad_sem,
    gsend_sem,
    grecv_sem,
    usend_sem,
    urecv_sem,
    psend_sem,
    precv_sem,
    tsend_sem,
    trecv_sem,
):
    mats, block_rows, block_cols, width = dims
    side = n * SLAB
    stripe = mats * block_rows * SLAB
    me = lax.axis_index("dp")
    mine = lax.axis_index("mp")
    xs = 4 if n >= 8 else 1
    zs = n // (2 * xs)
    plane = lax.div(me, 2 * xs)
    x = lax.rem(lax.div(me, 2), xs)
    core = lax.rem(me, 2)
    planes = [lax.rem(plane + i, zs) * (2 * xs) for i in range(zs)]
    columns = [lax.rem(x + i, xs) * 2 for i in range(xs)]

    route = [(c, i, j) for c in (1, 0) for i in range(xs) for j in far_first(zs)]

    def fan_out(start, places):
        for c, i, j in places:
            if i or j:
                start(planes[j] + columns[i] + c)
            else:
                pl.when(core != c)(functools.partial(start, planes[j] + columns[i] + c))


    pairs = [
        (slot_hbm, slot),
        (lbasis_hbm, lbasis),
        (rbasis_hbm, rbasis),
        (first_hbm, first),
        (second_hbm, second),
        (left_hbm, left),
        (right_hbm, right),
        (weights_hbm, weights),
    ]
    loads = [pltpu.make_async_copy(a, b, load_sem.at[i]) for i, (a, b) in enumerate(pairs)]
    per_col = mats * block_rows
    grad_loads = [
        pltpu.make_async_copy(
            grads_hbm.at[:, :, pl.ds(c * width, width)],
            grads.at[pl.ds(c * per_col, per_col)],
            grad_sem.at[c],
        )
        for c in range(block_cols)
    ]
    loads[0].start()
    for load in grad_loads:
        load.start()

    barrier = pltpu.get_barrier_semaphore()

    def greet(k, carry):
        pl.semaphore_signal(
            barrier, inc=1, device_id=(lax.rem(me + k, n), mine), device_id_type=MESH
        )
        return carry

    lax.fori_loop(1, n, greet, 0)
    sheet = [
        (planes[0] + columns[i] + 1, lax.rem(mine + j, groups))
        for j in range(groups)
        for i in range(xs)
    ]
    pillar = [planes[i] + columns[0] + c for i in range(zs) for c in (1, 0)][1:]
    for j in range(1, groups):
        for i in range(xs):
            for c in range(2):
                pl.semaphore_signal(
                    barrier,
                    inc=1,
                    device_id=(planes[0] + columns[i] + c, lax.rem(mine + j, groups)),
                    device_id_type=MESH,
                )

    loads[0].wait()
    for load in grad_loads:
        load.wait()
    for load in loads[1:]:
        load.start()

    def stage(s, carry):
        block = slot[s]
        c = lax.rem(block, block_cols)
        rest = lax.div(block, block_cols)
        gsend[s] = grads[c * per_col + rest]
        return carry

    lax.fori_loop(0, n, stage, 0, unroll=4)

    pl.semaphore_wait(barrier, n - 1 + (groups - 1) * xs * 2)

    def send_grad(peer):
        pltpu.make_async_remote_copy(
            src_ref=gsend.at[peer],
            dst_ref=gbuf.at[me],
            send_sem=gsend_sem,
            recv_sem=grecv_sem,
            device_id=(peer, mine),
            device_id_type=MESH,
        ).start()

    fan_out(send_grad, route)
    gbuf[me] = gsend[me]

    lanes = lax.broadcasted_iota(jnp.int32, (SLAB, side), 1)
    rows = lax.broadcasted_iota(jnp.int32, (SLAB, side), 0)

    def pick(s, carry):
        block = slot[s]
        c = lax.rem(block, block_cols)
        rest = lax.div(block, block_cols)
        base = c * stripe + rest * SLAB
        onehot[s] = (lanes - rows == base).astype(F32)
        return carry

    lax.fori_loop(0, n, pick, 0)
    onehot_t[...] = onehot[...].reshape(side, side).T.astype(BF16)
    loads[1].wait()
    lbasis_t[...] = lbasis[...].reshape(side, side).T

    for load in loads[2:5]:
        load.wait()

    all_of(gbuf, n - 1, grecv_sem).wait()
    grad = gbuf[...].reshape(side, width)
    half = mm(lbasis_t[...], grad).astype(BF16)
    rotated = mm(half, rbasis[...])
    new_first = beta_one * first[...] + (1.0 - beta_one) * rotated
    new_second = beta_two * second[...] + (1.0 - beta_two) * rotated * rotated
    first_out[...] = new_first
    second_out[...] = new_second
    normal = (new_first / first_fix / (jnp.sqrt(new_second / second_fix) + adam_eps)).astype(BF16)
    back = mm(lbasis[...].reshape(side, side), normal).astype(BF16)

    def send_update(peer):
        pltpu.make_async_remote_copy(
            src_ref=usend.at[peer],
            dst_ref=ubuf.at[me],
            send_sem=usend_sem,
            recv_sem=urecv_sem,
            device_id=(peer, mine),
            device_id_type=MESH,
        ).start()

    update = mm_t(back, rbasis[...]).astype(BF16)
    usend[...] = update.reshape(n, SLAB, width)
    wide = update.astype(F32)
    part = jnp.sum(wide * wide, axis=0, keepdims=True)
    lanes = sum(part[:, i * 128 : (i + 1) * 128] for i in range(width // 128))
    spot = (mine * xs + x) * 2 + core
    parts[spot] = lanes

    def send_part(there):
        pltpu.make_async_remote_copy(
            src_ref=parts.at[spot],
            dst_ref=parts.at[spot],
            send_sem=psend_sem,
            recv_sem=precv_sem,
            device_id=there,
            device_id_type=MESH,
        ).start()

    pl.when(core == 0)(functools.partial(send_part, sheet[0]))
    for there in sheet[1:]:
        send_part(there)
    fan_out(send_update, [(c, i, j) for i in range(xs) for j in far_first(zs) for c in (1, 0)])
    ubuf[me] = usend[me]

    loads[5].wait()
    loads[6].wait()
    new_left = stat_decay * left[...] + (1.0 - stat_decay) * mm_t(grad, grad)
    left_out[...] = new_left
    new_right = stat_decay * right[...] + (1.0 - stat_decay) * mm(grad.T, grad)
    right_out[...] = new_right

    left_new, right_new = orthogonalize(
        [
            mm(left_out[...].astype(BF16), lbasis[...].reshape(side, side)),
            mm(right_out[...].astype(BF16), rbasis[...]),
        ]
    )
    lnext_out[...] = left_new
    rnext_out[...] = right_new

    @pl.when(core == 1)
    def _():
        all_of(parts, 2 * len(sheet) - 1, precv_sem).wait()
        totals[plane] = jnp.sum(parts[...], axis=0)
        for there in pillar:
            pltpu.make_async_remote_copy(
                src_ref=totals.at[plane],
                dst_ref=totals.at[plane],
                send_sem=tsend_sem,
                recv_sem=trecv_sem,
                device_id=(there, mine),
                device_id_type=MESH,
            ).start()
        all_of(totals, zs - 1, trecv_sem).wait()

    @pl.when(core == 0)
    def _():
        all_of(totals, zs, trecv_sem).wait()

    loads[7].wait()
    all_of(gsend, n - 1, gsend_sem).wait()
    all_of(usend, n - 1, usend_sem).wait()

    all_of(parts, len(sheet) - 1, psend_sem).wait()

    @pl.when(core == 1)
    def _():
        all_of(parts, len(pillar), tsend_sem).wait()

    @pl.when(core == 0)
    def _():
        all_of(parts, 1, psend_sem).wait()

    all_of(ubuf, n - 1, urecv_sem).wait()


def store_kernel(dims, *refs):
    mats, block_rows, block_cols, width = dims
    stripe = mats * block_rows * SLAB
    done, (ubuf, onehot_t, weights, totals), rest = refs[:6], refs[6:10], refs[10:]
    step_hbm, outs, (step, sems) = rest[0], rest[1:7], rest[7:]
    copies = [pltpu.make_async_copy(a, b, sems.at[i]) for i, (a, b) in enumerate(zip(done, outs))]
    for copy in copies:
        copy.start()
    n = ubuf.shape[0]
    total = jnp.sum(totals[...])
    scale = jnp.minimum(1.0, clip_rms / jnp.sqrt(total / float(MATS * D * QW) + 1e-12))
    returned = ubuf[...].reshape(n * SLAB, width)
    for c in range(block_cols):
        placed = mm(onehot_t[c * stripe : (c + 1) * stripe, :], returned)
        at = slice(c * width, (c + 1) * width)
        step[:, at] = (scale * placed + decay_weight * weights[:, at].astype(F32)).astype(BF16)
    last = pltpu.make_async_copy(step, step_hbm, sems.at[6])
    last.start()
    for copy in copies:
        copy.wait()
    last.wait()


def body(n, groups, grads, weights, slot_block, first, second, left, right, lbasis, rbasis):
    mats, rows, cols = grads.shape
    side, width = first.shape[-2:]
    block_rows = rows // SLAB
    block_cols = cols // width
    dims = (mats, block_rows, block_cols, width)
    vmem = pltpu.VMEM
    xs = 4 if n >= 8 else 1
    zs = n // (2 * xs)
    dma = pltpu.SemaphoreType.DMA
    flat = (mats * rows, cols)
    shape = jax.ShapeDtypeStruct
    owned = [
        shape((side, width), F32),
        shape((side, width), F32),
        shape((side, side), F32),
        shape((width, width), F32),
        shape((side, side), BF16),
        shape((width, width), BF16),
    ]
    passed = [
        shape((n, SLAB, width), BF16),
        shape((side, side), BF16),
        shape(flat, BF16),
        shape((zs, 1, 128), F32),
    ]
    here = pl.BlockSpec(memory_space=pltpu.VMEM)
    away = pl.BlockSpec(memory_space=pltpu.HBM)
    results = pl.pallas_call(
        functools.partial(exchange_kernel, n, groups, dims),
        out_shape=owned + passed,
        in_specs=[away] * 9,
        out_specs=[here] * 10,
        scratch_shapes=[
            pltpu.SMEM((n,), jnp.int32),
            vmem((n, SLAB, width), BF16),
            vmem((side, width), F32),
            vmem((side, width), F32),
            vmem((side, side), F32),
            vmem((width, width), F32),
            vmem((n, SLAB, side), BF16),
            vmem((width, width), BF16),
            vmem((n, SLAB, side), F32),
            vmem((side, side), BF16),
            vmem((n, SLAB, width), BF16),
            vmem((n, SLAB, width), BF16),
            vmem((n, SLAB, width), BF16),
            vmem((2 * groups * xs, 1, 128), F32),
            dma((8,)),
            dma((block_cols,)),
            dma,
            dma,
            dma,
            dma,
            dma,
            dma,
            dma,
            dma,
        ],
        compiler_params=pltpu.CompilerParams(
            collective_id=0, has_side_effects=True, vmem_limit_bytes=40 * 1024 * 1024
        ),
    )(
        *[
            pltpu.with_memory_space_constraint(x, pltpu.HBM)
            for x in (
                slot_block,
                grads.reshape(mats * block_rows, SLAB, cols),
                weights.reshape(flat),
                first[0, 0],
                second[0, 0],
                left[0, 0],
                right[0, 0],
                lbasis[0, 0].reshape(n, SLAB, side),
                rbasis[0, 0],
            )
        ]
    )
    stored = pl.pallas_call(
        functools.partial(store_kernel, dims),
        out_shape=[shape(flat, BF16)] + owned,
        in_specs=[here] * 10,
        out_specs=[away] * 7,
        scratch_shapes=[vmem(flat, BF16), dma((7,))],
        compiler_params=pltpu.CompilerParams(vmem_limit_bytes=40 * 1024 * 1024),
    )(*results)
    return (stored[0].reshape(grads.shape), *[r[None, None] for r in stored[1:]])


def solution(mesh):
    owned = P("mp", "dp", None, None)
    rows = P(None, "dp", "mp")
    return jax.shard_map(
        functools.partial(body, mesh.shape["dp"], mesh.shape["mp"]),
        mesh=mesh,
        in_specs=(rows, rows, P()) + (owned,) * 6,
        out_specs=(rows,) + (owned,) * 6,
        check_vma=False,
    )
```

```python
import functools

import jax
import jax.numpy as jnp
from jax import lax
from jax.experimental import pallas as pl
from jax.experimental.pallas import tpu as pltpu
from jax.sharding import PartitionSpec as P

D = 4096
QW = 8192
MATS = 2
NS_STEPS = 2
beta_one = 0.9
beta_two = 0.95
stat_decay = 0.95
adam_eps = 1e-08
clip_rms = 0.2
decay_weight = 0.2
first_fix = 1.0 - 0.9**10
second_fix = 1.0 - 0.95**10
margin = 1.25

MESH = pl.DeviceIdType.MESH
F32 = jnp.float32
BF16 = jnp.bfloat16
SLAB = 8


def mm(a, b):
    return jnp.dot(a, b, preferred_element_type=F32)


def mm_t(a, b):
    return lax.dot_general(a, b, (((1,), (1,)), ((), ())), preferred_element_type=F32)


def orthogonalize(products):
    currents = []
    for product in products:
        norm_value = jnp.sqrt(jnp.sum(product * product) + 1e-12)
        factor = float(product.shape[0]) ** 0.5 / margin
        currents.append((product * (factor / norm_value)).astype(BF16))
    for turn in range(NS_STEPS):
        squares = [mm_t(x, x).astype(BF16) for x in currents]
        moved = [mm(s, x) for s, x in zip(squares, currents)]
        currents = [
            (1.5 * x.astype(F32) - 0.5 * m).astype(BF16) for x, m in zip(currents, moved)
        ]
    return currents


def far_first(zs):
    return sorted(range(zs), key=lambda j: (abs(2 * j - zs), j))


def all_of(ref, count, sem):
    part = ref.at[pl.ds(0, count)]
    return pltpu.make_async_copy(part, part, sem)


def exchange_kernel(
    n,
    groups,
    dims,
    slot_hbm,
    grads_hbm,
    weights_hbm,
    first_hbm,
    second_hbm,
    left_hbm,
    right_hbm,
    lbasis_hbm,
    rbasis_hbm,
    first_out,
    second_out,
    left_out,
    right_out,
    lnext_out,
    rnext_out,
    ubuf,
    onehot_t,
    weights,
    totals,
    slot,
    grads,
    first,
    second,
    left,
    right,
    lbasis,
    rbasis,
    onehot,
    lbasis_t,
    gsend,
    gbuf,
    usend,
    parts,
    mate_sem,
    load_sem,
    grad_sem,
    gsend_sem,
    grecv_sem,
    usend_sem,
    urecv_sem,
    psend_sem,
    precv_sem,
    tsend_sem,
    trecv_sem,
):
    mats, block_rows, block_cols, width = dims
    side = n * SLAB
    stripe = mats * block_rows * SLAB
    me = lax.axis_index("dp")
    mine = lax.axis_index("mp")
    xs = 4 if n >= 8 else 1
    zs = n // (2 * xs)
    plane = lax.div(me, 2 * xs)
    x = lax.rem(lax.div(me, 2), xs)
    core = lax.rem(me, 2)
    planes = [lax.rem(plane + i, zs) * (2 * xs) for i in range(zs)]
    columns = [lax.rem(x + i, xs) * 2 for i in range(xs)]

    def hops(i, j):
        return min(i, xs - i) + min(j, zs - j)

    spread = sorted(((i, j) for i in range(xs) for j in range(zs)), key=lambda p: -hops(*p))

    def fan_out(start, places):
        for c, i, j in places:
            if i or j:
                start(planes[j] + columns[i] + c)
            else:
                pl.when(core != c)(functools.partial(start, planes[j] + columns[i] + c))


    sheet = [
        (planes[0] + columns[i] + 1, lax.rem(mine + j, groups))
        for j in range(groups)
        for i in range(xs)
    ]
    pillar = [planes[j] + columns[0] + c for j in far_first(zs) for c in (1, 0) if j or not c]
    barrier = pltpu.get_barrier_semaphore()

    def greet(dp, mp):
        pl.semaphore_signal(barrier, inc=1, device_id=(dp, mp), device_id_type=MESH)

    near = [p for p in spread if min(p[1], zs - p[1]) <= min(1, zs // 2 - 1)]
    far = [p for p in spread if p not in near]
    for i, j in far:
        greet(planes[j] + columns[i], mine)
    for i, j in near:
        if i or j:
            greet(planes[j] + columns[i] + 1, mine)
    pl.when(core == 0)(functools.partial(greet, me + 1, mine))

    @pl.when(core == 1)
    def _():
        greet(me - 1, mine)
        for k, (there, group) in enumerate(sheet):
            if k >= xs:
                greet(there - 1, group)

    pairs = [
        (slot_hbm, slot),
        (lbasis_hbm, lbasis),
        (rbasis_hbm, rbasis),
        (first_hbm, first),
        (second_hbm, second),
        (left_hbm, left),
        (right_hbm, right),
        (weights_hbm, weights),
    ]
    loads = [pltpu.make_async_copy(a, b, load_sem.at[i]) for i, (a, b) in enumerate(pairs)]
    per_col = mats * block_rows
    grad_loads = [
        pltpu.make_async_copy(
            grads_hbm.at[:, :, pl.ds(c * width, width)],
            grads.at[pl.ds(c * per_col, per_col)],
            grad_sem.at[c],
        )
        for c in range(block_cols)
    ]
    loads[0].start()
    for load in grad_loads:
        load.start()

    loads[0].wait()
    for load in grad_loads:
        load.wait()
    for load in loads[1:]:
        load.start()

    def stage(s, carry):
        block = slot[s]
        c = lax.rem(block, block_cols)
        rest = lax.div(block, block_cols)
        gsend[s] = grads[c * per_col + rest]
        return carry

    lax.fori_loop(0, n, stage, 0, unroll=4)

    def send_grad(peer):
        pltpu.make_async_remote_copy(
            src_ref=gsend.at[peer],
            dst_ref=gbuf.at[me],
            send_sem=gsend_sem,
            recv_sem=grecv_sem,
            device_id=(peer, mine),
            device_id_type=MESH,
        ).start()

    def tell_mate():
        pl.semaphore_signal(
            mate_sem, inc=1, device_id=(me + 1 - 2 * core, mine), device_id_type=MESH
        )

    @pl.when(core == 1)
    def _():
        pl.semaphore_wait(barrier, 2 * len(near) - 1)
        tell_mate()

    pl.when(core == 0)(lambda: pl.semaphore_wait(mate_sem, 1))
    fan_out(send_grad, [(1, i, j) for i, j in near])

    @pl.when(core == 0)
    def _():
        pl.semaphore_wait(barrier, 2 * len(far) + 1 + (groups - 1) * xs)
        tell_mate()

    pl.when(core == 1)(lambda: pl.semaphore_wait(mate_sem, 1))
    fan_out(send_grad, [(c, i, j) for c in (1, 0) for i, j in spread if c == 0 or (i, j) in far])
    gbuf[me] = gsend[me]

    lanes = lax.broadcasted_iota(jnp.int32, (SLAB, side), 1)
    rows = lax.broadcasted_iota(jnp.int32, (SLAB, side), 0)

    def pick(s, carry):
        block = slot[s]
        c = lax.rem(block, block_cols)
        rest = lax.div(block, block_cols)
        base = c * stripe + rest * SLAB
        onehot[s] = (lanes - rows == base).astype(F32)
        return carry

    lax.fori_loop(0, n, pick, 0)
    onehot_t[...] = onehot[...].reshape(side, side).T.astype(BF16)
    loads[1].wait()
    lbasis_t[...] = lbasis[...].reshape(side, side).T

    for load in loads[2:5]:
        load.wait()

    all_of(gbuf, n - 1, grecv_sem).wait()
    grad = gbuf[...].reshape(side, width)
    half = mm(lbasis_t[...], grad).astype(BF16)
    rotated = mm(half, rbasis[...])
    new_first = beta_one * first[...] + (1.0 - beta_one) * rotated
    new_second = beta_two * second[...] + (1.0 - beta_two) * rotated * rotated
    first_out[...] = new_first
    second_out[...] = new_second
    normal = (new_first / first_fix / (jnp.sqrt(new_second / second_fix) + adam_eps)).astype(BF16)
    back = mm(lbasis[...].reshape(side, side), normal).astype(BF16)

    def send_update(peer):
        pltpu.make_async_remote_copy(
            src_ref=usend.at[peer],
            dst_ref=ubuf.at[me],
            send_sem=usend_sem,
            recv_sem=urecv_sem,
            device_id=(peer, mine),
            device_id_type=MESH,
        ).start()

    update = mm_t(back, rbasis[...]).astype(BF16)
    usend[...] = update.reshape(n, SLAB, width)
    wide = update.astype(F32)
    part = jnp.sum(wide * wide, axis=0, keepdims=True)
    lanes = sum(part[:, i * 128 : (i + 1) * 128] for i in range(width // 128))
    spot = (mine * xs + x) * 2 + core
    parts[spot] = lanes

    def send_part(there):
        pltpu.make_async_remote_copy(
            src_ref=parts.at[spot],
            dst_ref=parts.at[spot],
            send_sem=psend_sem,
            recv_sem=precv_sem,
            device_id=there,
            device_id_type=MESH,
        ).start()

    for k in sorted(range(1, len(sheet)), key=lambda k: -hops(k % xs, 0) - min(k // xs, groups - k // xs)):
        send_part(sheet[k])
    pl.when(core == 0)(functools.partial(send_part, sheet[0]))
    fan_out(send_update, [(c, i, j) for i in range(xs) for j in far_first(zs) for c in (1, 0)])
    ubuf[me] = usend[me]

    loads[5].wait()
    loads[6].wait()
    new_left = stat_decay * left[...] + (1.0 - stat_decay) * mm_t(grad, grad)
    left_out[...] = new_left
    new_right = stat_decay * right[...] + (1.0 - stat_decay) * mm(grad.T, grad)
    right_out[...] = new_right

    left_new, right_new = orthogonalize(
        [
            mm(left_out[...].astype(BF16), lbasis[...].reshape(side, side)),
            mm(right_out[...].astype(BF16), rbasis[...]),
        ]
    )
    lnext_out[...] = left_new
    rnext_out[...] = right_new

    @pl.when(core == 1)
    def _():
        all_of(parts, 2 * len(sheet) - 1, precv_sem).wait()
        totals[plane] = jnp.sum(parts[...], axis=0)
        for there in pillar:
            pltpu.make_async_remote_copy(
                src_ref=totals.at[plane],
                dst_ref=totals.at[plane],
                send_sem=tsend_sem,
                recv_sem=trecv_sem,
                device_id=(there, mine),
                device_id_type=MESH,
            ).start()
        all_of(totals, zs - 1, trecv_sem).wait()

    @pl.when(core == 0)
    def _():
        all_of(totals, zs, trecv_sem).wait()

    loads[7].wait()
    all_of(gsend, n - 1, gsend_sem).wait()
    all_of(usend, n - 1, usend_sem).wait()

    all_of(parts, len(sheet) - 1, psend_sem).wait()

    @pl.when(core == 1)
    def _():
        all_of(parts, len(pillar), tsend_sem).wait()

    @pl.when(core == 0)
    def _():
        all_of(parts, 1, psend_sem).wait()

    all_of(ubuf, n - 1, urecv_sem).wait()


def store_kernel(dims, *refs):
    mats, block_rows, block_cols, width = dims
    stripe = mats * block_rows * SLAB
    done, (ubuf, onehot_t, weights, totals), rest = refs[:6], refs[6:10], refs[10:]
    step_hbm, outs, (step, sems) = rest[0], rest[1:7], rest[7:]
    copies = [pltpu.make_async_copy(a, b, sems.at[i]) for i, (a, b) in enumerate(zip(done, outs))]
    for copy in copies:
        copy.start()
    n = ubuf.shape[0]
    total = jnp.sum(totals[...])
    scale = jnp.minimum(1.0, clip_rms / jnp.sqrt(total / float(MATS * D * QW) + 1e-12))
    returned = ubuf[...].reshape(n * SLAB, width)
    for c in range(block_cols):
        placed = mm(onehot_t[c * stripe : (c + 1) * stripe, :], returned)
        at = slice(c * width, (c + 1) * width)
        step[:, at] = (scale * placed + decay_weight * weights[:, at].astype(F32)).astype(BF16)
    last = pltpu.make_async_copy(step, step_hbm, sems.at[6])
    last.start()
    for copy in copies:
        copy.wait()
    last.wait()


def body(n, groups, grads, weights, slot_block, first, second, left, right, lbasis, rbasis):
    mats, rows, cols = grads.shape
    side, width = first.shape[-2:]
    block_rows = rows // SLAB
    block_cols = cols // width
    dims = (mats, block_rows, block_cols, width)
    vmem = pltpu.VMEM
    xs = 4 if n >= 8 else 1
    zs = n // (2 * xs)
    dma = pltpu.SemaphoreType.DMA
    flat = (mats * rows, cols)
    shape = jax.ShapeDtypeStruct
    owned = [
        shape((side, width), F32),
        shape((side, width), F32),
        shape((side, side), F32),
        shape((width, width), F32),
        shape((side, side), BF16),
        shape((width, width), BF16),
    ]
    passed = [
        shape((n, SLAB, width), BF16),
        shape((side, side), BF16),
        shape(flat, BF16),
        shape((zs, 1, 128), F32),
    ]
    here = pl.BlockSpec(memory_space=pltpu.VMEM)
    away = pl.BlockSpec(memory_space=pltpu.HBM)
    results = pl.pallas_call(
        functools.partial(exchange_kernel, n, groups, dims),
        out_shape=owned + passed,
        in_specs=[away] * 9,
        out_specs=[here] * 10,
        scratch_shapes=[
            pltpu.SMEM((n,), jnp.int32),
            vmem((n, SLAB, width), BF16),
            vmem((side, width), F32),
            vmem((side, width), F32),
            vmem((side, side), F32),
            vmem((width, width), F32),
            vmem((n, SLAB, side), BF16),
            vmem((width, width), BF16),
            vmem((n, SLAB, side), F32),
            vmem((side, side), BF16),
            vmem((n, SLAB, width), BF16),
            vmem((n, SLAB, width), BF16),
            vmem((n, SLAB, width), BF16),
            vmem((2 * groups * xs, 1, 128), F32),
            pltpu.SemaphoreType.REGULAR,
            dma((8,)),
            dma((block_cols,)),
            dma,
            dma,
            dma,
            dma,
            dma,
            dma,
            dma,
            dma,
        ],
        compiler_params=pltpu.CompilerParams(
            collective_id=0, has_side_effects=True, vmem_limit_bytes=40 * 1024 * 1024
        ),
    )(
        *[
            pltpu.with_memory_space_constraint(x, pltpu.HBM)
            for x in (
                slot_block,
                grads.reshape(mats * block_rows, SLAB, cols),
                weights.reshape(flat),
                first[0, 0],
                second[0, 0],
                left[0, 0],
                right[0, 0],
                lbasis[0, 0].reshape(n, SLAB, side),
                rbasis[0, 0],
            )
        ]
    )
    stored = pl.pallas_call(
        functools.partial(store_kernel, dims),
        out_shape=[shape(flat, BF16)] + owned,
        in_specs=[here] * 10,
        out_specs=[away] * 7,
        scratch_shapes=[vmem(flat, BF16), dma((7,))],
        compiler_params=pltpu.CompilerParams(vmem_limit_bytes=40 * 1024 * 1024),
    )(*results)
    return (stored[0].reshape(grads.shape), *[r[None, None] for r in stored[1:]])


def solution(mesh):
    owned = P("mp", "dp", None, None)
    rows = P(None, "dp", "mp")
    return jax.shard_map(
        functools.partial(body, mesh.shape["dp"], mesh.shape["mp"]),
        mesh=mesh,
        in_specs=(rows, rows, P()) + (owned,) * 6,
        out_specs=(rows,) + (owned,) * 6,
        check_vma=False,
    )
```

```python
import functools

import jax
import jax.numpy as jnp
from jax import lax
from jax.experimental import pallas as pl
from jax.experimental.pallas import tpu as pltpu
from jax.sharding import PartitionSpec as P

D = 4096
QW = 8192
MATS = 2
NS_STEPS = 2
beta_one = 0.9
beta_two = 0.95
stat_decay = 0.95
adam_eps = 1e-08
clip_rms = 0.2
decay_weight = 0.2
first_fix = 1.0 - 0.9**10
second_fix = 1.0 - 0.95**10
margin = 1.25

MESH = pl.DeviceIdType.MESH
F32 = jnp.float32
BF16 = jnp.bfloat16
SLAB = 8


def mm(a, b):
    return jnp.dot(a, b, preferred_element_type=F32)


def mm_t(a, b):
    return lax.dot_general(a, b, (((1,), (1,)), ((), ())), preferred_element_type=F32)


def orthogonalize(products):
    currents = []
    for product in products:
        norm_value = jnp.sqrt(jnp.sum(product * product) + 1e-12)
        factor = float(product.shape[0]) ** 0.5 / margin
        currents.append((product * (factor / norm_value)).astype(BF16))
    for turn in range(NS_STEPS):
        squares = [mm_t(x, x).astype(BF16) for x in currents]
        moved = [mm(s, x) for s, x in zip(squares, currents)]
        currents = [
            (1.5 * x.astype(F32) - 0.5 * m).astype(BF16) for x, m in zip(currents, moved)
        ]
    return currents


def far_first(zs):
    return sorted(range(zs), key=lambda j: (abs(2 * j - zs), j))


def all_of(ref, count, sem):
    part = ref.at[pl.ds(0, count)]
    return pltpu.make_async_copy(part, part, sem)


def exchange_kernel(
    n,
    groups,
    dims,
    slot_hbm,
    grads_hbm,
    weights_hbm,
    first_hbm,
    second_hbm,
    left_hbm,
    right_hbm,
    lbasis_hbm,
    rbasis_hbm,
    first_out,
    second_out,
    left_out,
    right_out,
    lnext_out,
    rnext_out,
    ubuf,
    onehot_t,
    weights,
    totals,
    slot,
    grads,
    first,
    second,
    left,
    right,
    lbasis,
    rbasis,
    onehot,
    lbasis_t,
    gsend,
    gbuf,
    usend,
    parts,
    mate_sem,
    load_sem,
    grad_sem,
    gsend_sem,
    grecv_sem,
    usend_sem,
    urecv_sem,
    psend_sem,
    precv_sem,
    tsend_sem,
    trecv_sem,
):
    mats, block_rows, block_cols, width = dims
    side = n * SLAB
    stripe = mats * block_rows * SLAB
    me = lax.axis_index("dp")
    mine = lax.axis_index("mp")
    xs = 4 if n >= 8 else 1
    zs = n // (2 * xs)
    plane = lax.div(me, 2 * xs)
    x = lax.rem(lax.div(me, 2), xs)
    core = lax.rem(me, 2)
    planes = [lax.rem(plane + i, zs) * (2 * xs) for i in range(zs)]
    columns = [lax.rem(x + i, xs) * 2 for i in range(xs)]

    def hops(i, j):
        return min(i, xs - i) + min(j, zs - j)

    spread = sorted(((i, j) for i in range(xs) for j in range(zs)), key=lambda p: -hops(*p))

    def fan_out(start, places):
        for c, i, j in places:
            if i or j:
                start(planes[j] + columns[i] + c)
            else:
                pl.when(core != c)(functools.partial(start, planes[j] + columns[i] + c))


    sheet = [
        (planes[0] + columns[i] + 1, lax.rem(mine + j, groups))
        for j in range(groups)
        for i in range(xs)
    ]
    pillar = [planes[j] + columns[0] + c for j in far_first(zs) for c in (1, 0) if j or not c]
    barrier = pltpu.get_barrier_semaphore()

    def greet(dp, mp):
        pl.semaphore_signal(barrier, inc=1, device_id=(dp, mp), device_id_type=MESH)

    near = [p for p in spread if min(p[1], zs - p[1]) <= min(1, zs // 2 - 1)]
    far = [p for p in spread if p not in near]
    for i, j in far:
        greet(planes[j] + columns[i], mine)
    for i, j in near:
        if i or j:
            greet(planes[j] + columns[i] + 1, mine)
    pl.when(core == 0)(functools.partial(greet, me + 1, mine))

    @pl.when(core == 1)
    def _():
        greet(me - 1, mine)
        for k, (there, group) in enumerate(sheet):
            if k >= xs:
                greet(there - 1, group)

    pairs = [
        (slot_hbm, slot),
        (lbasis_hbm, lbasis),
        (rbasis_hbm, rbasis),
        (first_hbm, first),
        (second_hbm, second),
        (left_hbm, left),
        (right_hbm, right),
        (weights_hbm, weights),
    ]
    loads = [pltpu.make_async_copy(a, b, load_sem.at[i]) for i, (a, b) in enumerate(pairs)]
    per_col = mats * block_rows
    grad_loads = [
        pltpu.make_async_copy(
            grads_hbm.at[:, :, pl.ds(c * width, width)],
            grads.at[pl.ds(c * per_col, per_col)],
            grad_sem.at[c],
        )
        for c in range(block_cols)
    ]
    loads[0].start()
    for load in grad_loads:
        load.start()

    loads[0].wait()
    for load in grad_loads:
        load.wait()
    for load in loads[1:]:
        load.start()

    def stage(s, carry):
        block = slot[s]
        c = lax.rem(block, block_cols)
        rest = lax.div(block, block_cols)
        gsend[s] = grads[c * per_col + rest]
        return carry

    lax.fori_loop(0, n, stage, 0, unroll=4)

    def send_grad(peer):
        pltpu.make_async_remote_copy(
            src_ref=gsend.at[peer],
            dst_ref=gbuf.at[me],
            send_sem=gsend_sem,
            recv_sem=grecv_sem,
            device_id=(peer, mine),
            device_id_type=MESH,
        ).start()

    def tell_mate():
        pl.semaphore_signal(
            mate_sem, inc=1, device_id=(me + 1 - 2 * core, mine), device_id_type=MESH
        )

    @pl.when(core == 1)
    def _():
        pl.semaphore_wait(barrier, 2 * len(near) - 1)
        tell_mate()

    pl.when(core == 0)(lambda: pl.semaphore_wait(mate_sem, 1))
    fan_out(send_grad, [(c, i, j) for c in (1, 0) for i, j in near])

    @pl.when(core == 0)
    def _():
        pl.semaphore_wait(barrier, 2 * len(far) + 1 + (groups - 1) * xs)
        tell_mate()

    pl.when(core == 1)(lambda: pl.semaphore_wait(mate_sem, 1))
    fan_out(send_grad, [(c, i, j) for c in (1, 0) for i, j in far])
    gbuf[me] = gsend[me]

    lanes = lax.broadcasted_iota(jnp.int32, (SLAB, side), 1)
    rows = lax.broadcasted_iota(jnp.int32, (SLAB, side), 0)

    def pick(s, carry):
        block = slot[s]
        c = lax.rem(block, block_cols)
        rest = lax.div(block, block_cols)
        base = c * stripe + rest * SLAB
        onehot[s] = (lanes - rows == base).astype(F32)
        return carry

    lax.fori_loop(0, n, pick, 0)
    onehot_t[...] = onehot[...].reshape(side, side).T.astype(BF16)
    loads[1].wait()
    lbasis_t[...] = lbasis[...].reshape(side, side).T

    for load in loads[2:5]:
        load.wait()

    all_of(gbuf, n - 1, grecv_sem).wait()
    grad = gbuf[...].reshape(side, width)
    half = mm(lbasis_t[...], grad).astype(BF16)
    rotated = mm(half, rbasis[...])
    new_first = beta_one * first[...] + (1.0 - beta_one) * rotated
    new_second = beta_two * second[...] + (1.0 - beta_two) * rotated * rotated
    first_out[...] = new_first
    second_out[...] = new_second
    normal = (new_first / first_fix / (jnp.sqrt(new_second / second_fix) + adam_eps)).astype(BF16)
    back = mm(lbasis[...].reshape(side, side), normal).astype(BF16)

    def send_update(peer):
        pltpu.make_async_remote_copy(
            src_ref=usend.at[peer],
            dst_ref=ubuf.at[me],
            send_sem=usend_sem,
            recv_sem=urecv_sem,
            device_id=(peer, mine),
            device_id_type=MESH,
        ).start()

    update = mm_t(back, rbasis[...]).astype(BF16)
    usend[...] = update.reshape(n, SLAB, width)
    wide = update.astype(F32)
    part = jnp.sum(wide * wide, axis=0, keepdims=True)
    lanes = sum(part[:, i * 128 : (i + 1) * 128] for i in range(width // 128))
    spot = (mine * xs + x) * 2 + core
    parts[spot] = lanes

    def send_part(there):
        pltpu.make_async_remote_copy(
            src_ref=parts.at[spot],
            dst_ref=parts.at[spot],
            send_sem=psend_sem,
            recv_sem=precv_sem,
            device_id=there,
            device_id_type=MESH,
        ).start()

    for k in sorted(range(1, len(sheet)), key=lambda k: -hops(k % xs, 0) - min(k // xs, groups - k // xs)):
        send_part(sheet[k])
    pl.when(core == 0)(functools.partial(send_part, sheet[0]))
    fan_out(send_update, [(c, i, j) for i in range(xs) for j in far_first(zs) for c in (1, 0)])
    ubuf[me] = usend[me]

    loads[5].wait()
    loads[6].wait()
    new_left = stat_decay * left[...] + (1.0 - stat_decay) * mm_t(grad, grad)
    left_out[...] = new_left
    new_right = stat_decay * right[...] + (1.0 - stat_decay) * mm(grad.T, grad)
    right_out[...] = new_right

    left_new, right_new = orthogonalize(
        [
            mm(left_out[...].astype(BF16), lbasis[...].reshape(side, side)),
            mm(right_out[...].astype(BF16), rbasis[...]),
        ]
    )
    lnext_out[...] = left_new
    rnext_out[...] = right_new

    @pl.when(core == 1)
    def _():
        all_of(parts, 2 * len(sheet) - 1, precv_sem).wait()
        totals[plane] = jnp.sum(parts[...], axis=0)
        for there in pillar:
            pltpu.make_async_remote_copy(
                src_ref=totals.at[plane],
                dst_ref=totals.at[plane],
                send_sem=tsend_sem,
                recv_sem=trecv_sem,
                device_id=(there, mine),
                device_id_type=MESH,
            ).start()
        all_of(totals, zs - 1, trecv_sem).wait()

    @pl.when(core == 0)
    def _():
        all_of(totals, zs, trecv_sem).wait()

    loads[7].wait()
    all_of(gsend, n - 1, gsend_sem).wait()
    all_of(usend, n - 1, usend_sem).wait()

    all_of(parts, len(sheet) - 1, psend_sem).wait()

    @pl.when(core == 1)
    def _():
        all_of(parts, len(pillar), tsend_sem).wait()

    @pl.when(core == 0)
    def _():
        all_of(parts, 1, psend_sem).wait()

    all_of(ubuf, n - 1, urecv_sem).wait()


def store_kernel(dims, *refs):
    mats, block_rows, block_cols, width = dims
    stripe = mats * block_rows * SLAB
    done, (ubuf, onehot_t, weights, totals), rest = refs[:6], refs[6:10], refs[10:]
    step_hbm, outs, (step, sems) = rest[0], rest[1:7], rest[7:]
    copies = [pltpu.make_async_copy(a, b, sems.at[i]) for i, (a, b) in enumerate(zip(done, outs))]
    for copy in copies:
        copy.start()
    n = ubuf.shape[0]
    total = jnp.sum(totals[...])
    scale = jnp.minimum(1.0, clip_rms / jnp.sqrt(total / float(MATS * D * QW) + 1e-12))
    returned = ubuf[...].reshape(n * SLAB, width)
    for c in range(block_cols):
        placed = mm(onehot_t[c * stripe : (c + 1) * stripe, :], returned)
        at = slice(c * width, (c + 1) * width)
        step[:, at] = (scale * placed + decay_weight * weights[:, at].astype(F32)).astype(BF16)
    last = pltpu.make_async_copy(step, step_hbm, sems.at[6])
    last.start()
    for copy in copies:
        copy.wait()
    last.wait()


def body(n, groups, grads, weights, slot_block, first, second, left, right, lbasis, rbasis):
    mats, rows, cols = grads.shape
    side, width = first.shape[-2:]
    block_rows = rows // SLAB
    block_cols = cols // width
    dims = (mats, block_rows, block_cols, width)
    vmem = pltpu.VMEM
    xs = 4 if n >= 8 else 1
    zs = n // (2 * xs)
    dma = pltpu.SemaphoreType.DMA
    flat = (mats * rows, cols)
    shape = jax.ShapeDtypeStruct
    owned = [
        shape((side, width), F32),
        shape((side, width), F32),
        shape((side, side), F32),
        shape((width, width), F32),
        shape((side, side), BF16),
        shape((width, width), BF16),
    ]
    passed = [
        shape((n, SLAB, width), BF16),
        shape((side, side), BF16),
        shape(flat, BF16),
        shape((zs, 1, 128), F32),
    ]
    here = pl.BlockSpec(memory_space=pltpu.VMEM)
    away = pl.BlockSpec(memory_space=pltpu.HBM)
    results = pl.pallas_call(
        functools.partial(exchange_kernel, n, groups, dims),
        out_shape=owned + passed,
        in_specs=[away] * 9,
        out_specs=[here] * 10,
        scratch_shapes=[
            pltpu.SMEM((n,), jnp.int32),
            vmem((n, SLAB, width), BF16),
            vmem((side, width), F32),
            vmem((side, width), F32),
            vmem((side, side), F32),
            vmem((width, width), F32),
            vmem((n, SLAB, side), BF16),
            vmem((width, width), BF16),
            vmem((n, SLAB, side), F32),
            vmem((side, side), BF16),
            vmem((n, SLAB, width), BF16),
            vmem((n, SLAB, width), BF16),
            vmem((n, SLAB, width), BF16),
            vmem((2 * groups * xs, 1, 128), F32),
            pltpu.SemaphoreType.REGULAR,
            dma((8,)),
            dma((block_cols,)),
            dma,
            dma,
            dma,
            dma,
            dma,
            dma,
            dma,
            dma,
        ],
        compiler_params=pltpu.CompilerParams(
            collective_id=0, has_side_effects=True, vmem_limit_bytes=40 * 1024 * 1024
        ),
    )(
        *[
            pltpu.with_memory_space_constraint(x, pltpu.HBM)
            for x in (
                slot_block,
                grads.reshape(mats * block_rows, SLAB, cols),
                weights.reshape(flat),
                first[0, 0],
                second[0, 0],
                left[0, 0],
                right[0, 0],
                lbasis[0, 0].reshape(n, SLAB, side),
                rbasis[0, 0],
            )
        ]
    )
    stored = pl.pallas_call(
        functools.partial(store_kernel, dims),
        out_shape=[shape(flat, BF16)] + owned,
        in_specs=[here] * 10,
        out_specs=[away] * 7,
        scratch_shapes=[vmem(flat, BF16), dma((7,))],
        compiler_params=pltpu.CompilerParams(vmem_limit_bytes=40 * 1024 * 1024),
    )(*results)
    return (stored[0].reshape(grads.shape), *[r[None, None] for r in stored[1:]])


def solution(mesh):
    owned = P("mp", "dp", None, None)
    rows = P(None, "dp", "mp")
    return jax.shard_map(
        functools.partial(body, mesh.shape["dp"], mesh.shape["mp"]),
        mesh=mesh,
        in_specs=(rows, rows, P()) + (owned,) * 6,
        out_specs=(rows,) + (owned,) * 6,
        check_vma=False,
    )
```

```python
import functools

import jax
import jax.numpy as jnp
from jax import lax
from jax.experimental import pallas as pl
from jax.experimental.pallas import tpu as pltpu
from jax.sharding import PartitionSpec as P

D = 4096
QW = 8192
MATS = 2
NS_STEPS = 2
beta_one = 0.9
beta_two = 0.95
stat_decay = 0.95
adam_eps = 1e-08
clip_rms = 0.2
decay_weight = 0.2
first_fix = 1.0 - 0.9**10
second_fix = 1.0 - 0.95**10
margin = 1.25

MESH = pl.DeviceIdType.MESH
F32 = jnp.float32
BF16 = jnp.bfloat16
SLAB = 8


def mm(a, b):
    return jnp.dot(a, b, preferred_element_type=F32)


def mm_t(a, b):
    return lax.dot_general(a, b, (((1,), (1,)), ((), ())), preferred_element_type=F32)


def orthogonalize(products):
    currents = []
    for product in products:
        norm_value = jnp.sqrt(jnp.sum(product * product) + 1e-12)
        factor = float(product.shape[0]) ** 0.5 / margin
        currents.append((product * (factor / norm_value)).astype(BF16))
    for turn in range(NS_STEPS):
        squares = [mm_t(x, x).astype(BF16) for x in currents]
        moved = [mm(s, x) for s, x in zip(squares, currents)]
        currents = [
            (1.5 * x.astype(F32) - 0.5 * m).astype(BF16) for x, m in zip(currents, moved)
        ]
    return currents


def far_first(zs):
    return sorted(range(zs), key=lambda j: (abs(2 * j - zs), j))


def all_of(ref, count, sem):
    part = ref.at[pl.ds(0, count)]
    return pltpu.make_async_copy(part, part, sem)


def exchange_kernel(
    n,
    groups,
    dims,
    slot_hbm,
    grads_hbm,
    weights_hbm,
    first_hbm,
    second_hbm,
    left_hbm,
    right_hbm,
    lbasis_hbm,
    rbasis_hbm,
    first_out,
    second_out,
    left_out,
    right_out,
    lnext_out,
    rnext_out,
    ubuf,
    onehot_t,
    weights,
    totals,
    slot,
    grads,
    first,
    second,
    left,
    right,
    lbasis,
    rbasis,
    onehot,
    lbasis_t,
    gsend,
    gbuf,
    usend,
    parts,
    mate_sem,
    load_sem,
    grad_sem,
    gsend_sem,
    grecv_sem,
    usend_sem,
    urecv_sem,
    psend_sem,
    precv_sem,
    tsend_sem,
    trecv_sem,
):
    mats, block_rows, block_cols, width = dims
    side = n * SLAB
    stripe = mats * block_rows * SLAB
    me = lax.axis_index("dp")
    mine = lax.axis_index("mp")
    xs = 4 if n >= 8 else 1
    zs = n // (2 * xs)
    plane = lax.div(me, 2 * xs)
    x = lax.rem(lax.div(me, 2), xs)
    core = lax.rem(me, 2)
    planes = [lax.rem(plane + i, zs) * (2 * xs) for i in range(zs)]
    columns = [lax.rem(x + i, xs) * 2 for i in range(xs)]

    def hops(i, j):
        return min(i, xs - i) + min(j, zs - j)

    spread = sorted(((i, j) for i in range(xs) for j in range(zs)), key=lambda p: -hops(*p))

    def fan_out(start, places):
        for c, i, j in places:
            if i or j:
                start(planes[j] + columns[i] + c)
            else:
                pl.when(core != c)(functools.partial(start, planes[j] + columns[i] + c))


    sheet = [
        (planes[0] + columns[i] + 1, lax.rem(mine + j, groups))
        for j in range(groups)
        for i in range(xs)
    ]
    pillar = [planes[j] + columns[0] + c for j in far_first(zs) for c in (1, 0) if j or not c]
    barrier = pltpu.get_barrier_semaphore()

    def greet(dp, mp):
        pl.semaphore_signal(barrier, inc=1, device_id=(dp, mp), device_id_type=MESH)

    near = [p for p in spread if min(p[1], zs - p[1]) <= min(1, zs // 2 - 1)]
    far = [p for p in spread if p not in near]
    for i, j in far:
        greet(planes[j] + columns[i], mine)
    for i, j in near:
        if i or j:
            greet(planes[j] + columns[i] + 1, mine)
    pl.when(core == 0)(functools.partial(greet, me + 1, mine))

    @pl.when(core == 1)
    def _():
        greet(me - 1, mine)
        for k, (there, group) in enumerate(sheet):
            if k >= xs:
                greet(there - 1, group)

    pairs = [
        (slot_hbm, slot),
        (lbasis_hbm, lbasis),
        (rbasis_hbm, rbasis),
        (first_hbm, first),
        (second_hbm, second),
        (left_hbm, left),
        (right_hbm, right),
        (weights_hbm, weights),
    ]
    loads = [pltpu.make_async_copy(a, b, load_sem.at[i]) for i, (a, b) in enumerate(pairs)]
    per_col = mats * block_rows
    grad_loads = [
        pltpu.make_async_copy(
            grads_hbm.at[:, :, pl.ds(c * width, width)],
            grads.at[pl.ds(c * per_col, per_col)],
            grad_sem.at[c],
        )
        for c in range(block_cols)
    ]
    loads[0].start()
    for load in grad_loads:
        load.start()

    loads[0].wait()
    for load in grad_loads:
        load.wait()
    for load in loads[1:]:
        load.start()

    def stage(s, carry):
        block = slot[s]
        c = lax.rem(block, block_cols)
        rest = lax.div(block, block_cols)
        gsend[s] = grads[c * per_col + rest]
        return carry

    lax.fori_loop(0, n, stage, 0, unroll=4)

    def send_grad(peer):
        pltpu.make_async_remote_copy(
            src_ref=gsend.at[peer],
            dst_ref=gbuf.at[me],
            send_sem=gsend_sem,
            recv_sem=grecv_sem,
            device_id=(peer, mine),
            device_id_type=MESH,
        ).start()

    def tell_mate():
        pl.semaphore_signal(
            mate_sem, inc=1, device_id=(me + 1 - 2 * core, mine), device_id_type=MESH
        )

    @pl.when(core == 1)
    def _():
        pl.semaphore_wait(barrier, 2 * len(near) - 1)
        tell_mate()

    pl.when(core == 0)(lambda: pl.semaphore_wait(mate_sem, 1))
    fan_out(send_grad, [(c, i, j) for c in (1, 0) for i, j in near])

    @pl.when(core == 0)
    def _():
        pl.semaphore_wait(barrier, 2 * len(far) + 1 + (groups - 1) * xs)
        tell_mate()

    pl.when(core == 1)(lambda: pl.semaphore_wait(mate_sem, 1))
    fan_out(send_grad, [(c, i, j) for c in (1, 0) for i, j in far])
    gbuf[me] = gsend[me]

    lanes = lax.broadcasted_iota(jnp.int32, (SLAB, side), 1)
    rows = lax.broadcasted_iota(jnp.int32, (SLAB, side), 0)

    def pick(s, carry):
        block = slot[s]
        c = lax.rem(block, block_cols)
        rest = lax.div(block, block_cols)
        base = c * stripe + rest * SLAB
        onehot[s] = (lanes - rows == base).astype(F32)
        return carry

    lax.fori_loop(0, n, pick, 0)
    onehot_t[...] = onehot[...].reshape(side, side).T.astype(BF16)
    loads[1].wait()
    lbasis_t[...] = lbasis[...].reshape(side, side).T

    for load in loads[2:5]:
        load.wait()

    all_of(gbuf, n - 1, grecv_sem).wait()
    grad = gbuf[...].reshape(side, width)
    half = mm(lbasis_t[...], grad).astype(BF16)
    rotated = mm(half, rbasis[...])
    new_first = beta_one * first[...] + (1.0 - beta_one) * rotated
    new_second = beta_two * second[...] + (1.0 - beta_two) * rotated * rotated
    first_out[...] = new_first
    second_out[...] = new_second
    normal = (new_first / first_fix / (jnp.sqrt(new_second / second_fix) + adam_eps)).astype(BF16)
    back = mm(lbasis[...].reshape(side, side), normal).astype(BF16)

    def send_update(peer):
        pltpu.make_async_remote_copy(
            src_ref=usend.at[peer],
            dst_ref=ubuf.at[me],
            send_sem=usend_sem,
            recv_sem=urecv_sem,
            device_id=(peer, mine),
            device_id_type=MESH,
        ).start()

    update = mm_t(back, rbasis[...]).astype(BF16)
    usend[...] = update.reshape(n, SLAB, width)
    wide = update.astype(F32)
    part = jnp.sum(wide * wide, axis=0, keepdims=True)
    lanes = sum(part[:, i * 128 : (i + 1) * 128] for i in range(width // 128))
    spot = (mine * xs + x) * 2 + core
    parts[spot] = lanes

    def send_part(there):
        pltpu.make_async_remote_copy(
            src_ref=parts.at[spot],
            dst_ref=parts.at[spot],
            send_sem=psend_sem,
            recv_sem=precv_sem,
            device_id=there,
            device_id_type=MESH,
        ).start()

    for k in sorted(range(1, len(sheet)), key=lambda k: -hops(k % xs, 0) - min(k // xs, groups - k // xs)):
        send_part(sheet[k])
    pl.when(core == 0)(functools.partial(send_part, sheet[0]))
    fan_out(send_update, [(c, i, j) for i in sorted(range(xs), key=lambda i: -min(i, xs - i)) for j in far_first(zs) for c in (1, 0)])
    ubuf[me] = usend[me]

    loads[5].wait()
    loads[6].wait()
    new_left = stat_decay * left[...] + (1.0 - stat_decay) * mm_t(grad, grad)
    left_out[...] = new_left
    new_right = stat_decay * right[...] + (1.0 - stat_decay) * mm(grad.T, grad)
    right_out[...] = new_right

    left_new, right_new = orthogonalize(
        [
            mm(left_out[...].astype(BF16), lbasis[...].reshape(side, side)),
            mm(right_out[...].astype(BF16), rbasis[...]),
        ]
    )
    lnext_out[...] = left_new
    rnext_out[...] = right_new

    @pl.when(core == 1)
    def _():
        all_of(parts, 2 * len(sheet) - 1, precv_sem).wait()
        totals[plane] = jnp.sum(parts[...], axis=0)
        for there in pillar:
            pltpu.make_async_remote_copy(
                src_ref=totals.at[plane],
                dst_ref=totals.at[plane],
                send_sem=tsend_sem,
                recv_sem=trecv_sem,
                device_id=(there, mine),
                device_id_type=MESH,
            ).start()
        all_of(totals, zs - 1, trecv_sem).wait()

    @pl.when(core == 0)
    def _():
        all_of(totals, zs, trecv_sem).wait()

    loads[7].wait()
    all_of(gsend, n - 1, gsend_sem).wait()
    all_of(usend, n - 1, usend_sem).wait()

    all_of(parts, len(sheet) - 1, psend_sem).wait()

    @pl.when(core == 1)
    def _():
        all_of(parts, len(pillar), tsend_sem).wait()

    @pl.when(core == 0)
    def _():
        all_of(parts, 1, psend_sem).wait()

    all_of(ubuf, n - 1, urecv_sem).wait()


def store_kernel(dims, *refs):
    mats, block_rows, block_cols, width = dims
    stripe = mats * block_rows * SLAB
    done, (ubuf, onehot_t, weights, totals), rest = refs[:6], refs[6:10], refs[10:]
    step_hbm, outs, (step, sems) = rest[0], rest[1:7], rest[7:]
    copies = [pltpu.make_async_copy(a, b, sems.at[i]) for i, (a, b) in enumerate(zip(done, outs))]
    for copy in copies:
        copy.start()
    n = ubuf.shape[0]
    total = jnp.sum(totals[...])
    scale = jnp.minimum(1.0, clip_rms / jnp.sqrt(total / float(MATS * D * QW) + 1e-12))
    returned = ubuf[...].reshape(n * SLAB, width)
    for c in range(block_cols):
        placed = mm(onehot_t[c * stripe : (c + 1) * stripe, :], returned)
        at = slice(c * width, (c + 1) * width)
        step[:, at] = (scale * placed + decay_weight * weights[:, at].astype(F32)).astype(BF16)
    last = pltpu.make_async_copy(step, step_hbm, sems.at[6])
    last.start()
    for copy in copies:
        copy.wait()
    last.wait()


def body(n, groups, grads, weights, slot_block, first, second, left, right, lbasis, rbasis):
    mats, rows, cols = grads.shape
    side, width = first.shape[-2:]
    block_rows = rows // SLAB
    block_cols = cols // width
    dims = (mats, block_rows, block_cols, width)
    vmem = pltpu.VMEM
    xs = 4 if n >= 8 else 1
    zs = n // (2 * xs)
    dma = pltpu.SemaphoreType.DMA
    flat = (mats * rows, cols)
    shape = jax.ShapeDtypeStruct
    owned = [
        shape((side, width), F32),
        shape((side, width), F32),
        shape((side, side), F32),
        shape((width, width), F32),
        shape((side, side), BF16),
        shape((width, width), BF16),
    ]
    passed = [
        shape((n, SLAB, width), BF16),
        shape((side, side), BF16),
        shape(flat, BF16),
        shape((zs, 1, 128), F32),
    ]
    here = pl.BlockSpec(memory_space=pltpu.VMEM)
    away = pl.BlockSpec(memory_space=pltpu.HBM)
    results = pl.pallas_call(
        functools.partial(exchange_kernel, n, groups, dims),
        out_shape=owned + passed,
        in_specs=[away] * 9,
        out_specs=[here] * 10,
        scratch_shapes=[
            pltpu.SMEM((n,), jnp.int32),
            vmem((n, SLAB, width), BF16),
            vmem((side, width), F32),
            vmem((side, width), F32),
            vmem((side, side), F32),
            vmem((width, width), F32),
            vmem((n, SLAB, side), BF16),
            vmem((width, width), BF16),
            vmem((n, SLAB, side), F32),
            vmem((side, side), BF16),
            vmem((n, SLAB, width), BF16),
            vmem((n, SLAB, width), BF16),
            vmem((n, SLAB, width), BF16),
            vmem((2 * groups * xs, 1, 128), F32),
            pltpu.SemaphoreType.REGULAR,
            dma((8,)),
            dma((block_cols,)),
            dma,
            dma,
            dma,
            dma,
            dma,
            dma,
            dma,
            dma,
        ],
        compiler_params=pltpu.CompilerParams(
            collective_id=0, has_side_effects=True, vmem_limit_bytes=40 * 1024 * 1024
        ),
    )(
        *[
            pltpu.with_memory_space_constraint(x, pltpu.HBM)
            for x in (
                slot_block,
                grads.reshape(mats * block_rows, SLAB, cols),
                weights.reshape(flat),
                first[0, 0],
                second[0, 0],
                left[0, 0],
                right[0, 0],
                lbasis[0, 0].reshape(n, SLAB, side),
                rbasis[0, 0],
            )
        ]
    )
    stored = pl.pallas_call(
        functools.partial(store_kernel, dims),
        out_shape=[shape(flat, BF16)] + owned,
        in_specs=[here] * 10,
        out_specs=[away] * 7,
        scratch_shapes=[vmem(flat, BF16), dma((7,))],
        compiler_params=pltpu.CompilerParams(vmem_limit_bytes=40 * 1024 * 1024),
    )(*results)
    return (stored[0].reshape(grads.shape), *[r[None, None] for r in stored[1:]])


def solution(mesh):
    owned = P("mp", "dp", None, None)
    rows = P(None, "dp", "mp")
    return jax.shard_map(
        functools.partial(body, mesh.shape["dp"], mesh.shape["mp"]),
        mesh=mesh,
        in_specs=(rows, rows, P()) + (owned,) * 6,
        out_specs=(rows,) + (owned,) * 6,
        check_vma=False,
    )
```

```python
import functools

import jax
import jax.numpy as jnp
from jax import lax
from jax.experimental import pallas as pl
from jax.experimental.pallas import tpu as pltpu
from jax.sharding import PartitionSpec as P

D = 4096
QW = 8192
MATS = 2
NS_STEPS = 2
beta_one = 0.9
beta_two = 0.95
stat_decay = 0.95
adam_eps = 1e-08
clip_rms = 0.2
decay_weight = 0.2
first_fix = 1.0 - 0.9**10
second_fix = 1.0 - 0.95**10
margin = 1.25

MESH = pl.DeviceIdType.MESH
F32 = jnp.float32
BF16 = jnp.bfloat16
SLAB = 8


def mm(a, b):
    return jnp.dot(a, b, preferred_element_type=F32)


def mm_t(a, b):
    return lax.dot_general(a, b, (((1,), (1,)), ((), ())), preferred_element_type=F32)


def orthogonalize(products):
    currents = []
    for product in products:
        norm_value = jnp.sqrt(jnp.sum(product * product) + 1e-12)
        factor = float(product.shape[0]) ** 0.5 / margin
        currents.append((product * (factor / norm_value)).astype(BF16))
    for turn in range(NS_STEPS):
        squares = [mm_t(x, x).astype(BF16) for x in currents]
        moved = [mm(s, x) for s, x in zip(squares, currents)]
        currents = [
            (1.5 * x.astype(F32) - 0.5 * m).astype(BF16) for x, m in zip(currents, moved)
        ]
    return currents


def far_first(zs):
    return sorted(range(zs), key=lambda j: (abs(2 * j - zs), j))


def all_of(ref, count, sem):
    part = ref.at[pl.ds(0, count)]
    return pltpu.make_async_copy(part, part, sem)


def exchange_kernel(
    n,
    groups,
    dims,
    slot_hbm,
    grads_hbm,
    weights_hbm,
    first_hbm,
    second_hbm,
    left_hbm,
    right_hbm,
    lbasis_hbm,
    rbasis_hbm,
    first_out,
    second_out,
    left_out,
    right_out,
    lnext_out,
    rnext_out,
    ubuf,
    onehot_t,
    weights,
    totals,
    slot,
    grads,
    first,
    second,
    left,
    right,
    lbasis,
    rbasis,
    onehot,
    lbasis_t,
    gsend,
    gbuf,
    usend,
    parts,
    mate_sem,
    load_sem,
    grad_sem,
    gsend_sem,
    grecv_sem,
    usend_sem,
    urecv_sem,
    psend_sem,
    precv_sem,
    tsend_sem,
    trecv_sem,
):
    mats, block_rows, block_cols, width = dims
    side = n * SLAB
    stripe = mats * block_rows * SLAB
    me = lax.axis_index("dp")
    mine = lax.axis_index("mp")
    xs = 4 if n >= 8 else 1
    zs = n // (2 * xs)
    plane = lax.div(me, 2 * xs)
    x = lax.rem(lax.div(me, 2), xs)
    core = lax.rem(me, 2)
    planes = [lax.rem(plane + i, zs) * (2 * xs) for i in range(zs)]
    columns = [lax.rem(x + i, xs) * 2 for i in range(xs)]

    def hops(i, j):
        return min(i, xs - i) + min(j, zs - j)

    spread = sorted(((i, j) for i in range(xs) for j in range(zs)), key=lambda p: -hops(*p))

    def fan_out(start, places):
        for c, i, j in places:
            if i or j:
                start(planes[j] + columns[i] + c)
            else:
                pl.when(core != c)(functools.partial(start, planes[j] + columns[i] + c))


    sheet = [
        (planes[0] + columns[i] + 1, lax.rem(mine + j, groups))
        for j in range(groups)
        for i in range(xs)
    ]
    pillar = [planes[j] + columns[0] + c for j in far_first(zs) for c in (1, 0) if j or not c]
    barrier = pltpu.get_barrier_semaphore()

    def greet(dp, mp):
        pl.semaphore_signal(barrier, inc=1, device_id=(dp, mp), device_id_type=MESH)

    near = [p for p in spread if min(p[1], zs - p[1]) <= min(1, zs // 2 - 1)]
    far = [p for p in spread if p not in near]
    for i, j in far:
        greet(planes[j] + columns[i], mine)
    for i, j in near:
        if i or j:
            greet(planes[j] + columns[i] + 1, mine)
    pl.when(core == 0)(functools.partial(greet, me + 1, mine))

    @pl.when(core == 1)
    def _():
        greet(me - 1, mine)
        for k, (there, group) in enumerate(sheet):
            if k >= xs:
                greet(there - 1, group)

    pairs = [
        (slot_hbm, slot),
        (lbasis_hbm, lbasis),
        (rbasis_hbm, rbasis),
        (first_hbm, first),
        (second_hbm, second),
        (left_hbm, left),
        (right_hbm, right),
        (weights_hbm, weights),
    ]
    loads = [pltpu.make_async_copy(a, b, load_sem.at[i]) for i, (a, b) in enumerate(pairs)]
    per_col = mats * block_rows
    grad_loads = [
        pltpu.make_async_copy(
            grads_hbm.at[:, :, pl.ds(c * width, width)],
            grads.at[pl.ds(c * per_col, per_col)],
            grad_sem.at[c],
        )
        for c in range(block_cols)
    ]
    loads[0].start()
    for load in grad_loads:
        load.start()

    loads[0].wait()
    for load in grad_loads:
        load.wait()
    for load in loads[1:]:
        load.start()

    def stage(s, carry):
        block = slot[s]
        c = lax.rem(block, block_cols)
        rest = lax.div(block, block_cols)
        gsend[s] = grads[c * per_col + rest]
        return carry

    lax.fori_loop(0, n, stage, 0, unroll=4)

    def send_grad(peer):
        pltpu.make_async_remote_copy(
            src_ref=gsend.at[peer],
            dst_ref=gbuf.at[me],
            send_sem=gsend_sem,
            recv_sem=grecv_sem,
            device_id=(peer, mine),
            device_id_type=MESH,
        ).start()

    def tell_mate():
        pl.semaphore_signal(
            mate_sem, inc=1, device_id=(me + 1 - 2 * core, mine), device_id_type=MESH
        )

    @pl.when(core == 1)
    def _():
        pl.semaphore_wait(barrier, 2 * len(near) - 1)
        tell_mate()

    pl.when(core == 0)(lambda: pl.semaphore_wait(mate_sem, 1))
    fan_out(send_grad, [(c, i, j) for c in (1, 0) for i, j in near])

    @pl.when(core == 0)
    def _():
        pl.semaphore_wait(barrier, 2 * len(far) + 1 + (groups - 1) * xs)
        tell_mate()

    pl.when(core == 1)(lambda: pl.semaphore_wait(mate_sem, 1))
    fan_out(send_grad, [(c, i, j) for c in (1, 0) for i, j in far])
    gbuf[me] = gsend[me]

    lanes = lax.broadcasted_iota(jnp.int32, (SLAB, side), 1)
    rows = lax.broadcasted_iota(jnp.int32, (SLAB, side), 0)

    def pick(s, carry):
        block = slot[s]
        c = lax.rem(block, block_cols)
        rest = lax.div(block, block_cols)
        base = c * stripe + rest * SLAB
        onehot[s] = (lanes - rows == base).astype(F32)
        return carry

    lax.fori_loop(0, n, pick, 0)
    onehot_t[...] = onehot[...].reshape(side, side).T.astype(BF16)
    loads[1].wait()
    lbasis_t[...] = lbasis[...].reshape(side, side).T

    for load in loads[2:5]:
        load.wait()

    all_of(gbuf, n - 1, grecv_sem).wait()
    grad = gbuf[...].reshape(side, width)
    half = mm(lbasis_t[...], grad).astype(BF16)
    rotated = mm(half, rbasis[...])
    new_first = beta_one * first[...] + (1.0 - beta_one) * rotated
    new_second = beta_two * second[...] + (1.0 - beta_two) * rotated * rotated
    first_out[...] = new_first
    second_out[...] = new_second
    normal = (new_first / first_fix / (jnp.sqrt(new_second / second_fix) + adam_eps)).astype(BF16)
    back = mm(lbasis[...].reshape(side, side), normal).astype(BF16)

    def send_update(peer):
        pltpu.make_async_remote_copy(
            src_ref=usend.at[peer],
            dst_ref=ubuf.at[me],
            send_sem=usend_sem,
            recv_sem=urecv_sem,
            device_id=(peer, mine),
            device_id_type=MESH,
        ).start()

    update = mm_t(back, rbasis[...]).astype(BF16)
    usend[...] = update.reshape(n, SLAB, width)
    spot = (mine * xs + x) * 2 + core

    def send_parts():
        wide = usend[...].reshape(side, width).astype(F32)
        part = jnp.sum(wide * wide, axis=0, keepdims=True)
        parts[spot] = sum(part[:, i * 128 : (i + 1) * 128] for i in range(width // 128))
        for k in sorted(
            range(1, len(sheet)), key=lambda k: -hops(k % xs, 0) - min(k // xs, groups - k // xs)
        ):
            send_part(sheet[k])

    def send_part(there):
        pltpu.make_async_remote_copy(
            src_ref=parts.at[spot],
            dst_ref=parts.at[spot],
            send_sem=psend_sem,
            recv_sem=precv_sem,
            device_id=there,
            device_id_type=MESH,
        ).start()

    @pl.when(core == 0)
    def _():
        send_parts()
        send_part(sheet[0])

    fan_out(send_update, [(c, i, j) for i in range(xs) for j in far_first(zs) for c in (1, 0)])
    pl.when(core == 1)(send_parts)
    ubuf[me] = usend[me]

    loads[5].wait()
    loads[6].wait()
    new_left = stat_decay * left[...] + (1.0 - stat_decay) * mm_t(grad, grad)
    left_out[...] = new_left
    new_right = stat_decay * right[...] + (1.0 - stat_decay) * mm(grad.T, grad)
    right_out[...] = new_right

    left_new, right_new = orthogonalize(
        [
            mm(left_out[...].astype(BF16), lbasis[...].reshape(side, side)),
            mm(right_out[...].astype(BF16), rbasis[...]),
        ]
    )
    lnext_out[...] = left_new
    rnext_out[...] = right_new

    @pl.when(core == 1)
    def _():
        all_of(parts, 2 * len(sheet) - 1, precv_sem).wait()
        totals[plane] = jnp.sum(parts[...], axis=0)
        for there in pillar:
            pltpu.make_async_remote_copy(
                src_ref=totals.at[plane],
                dst_ref=totals.at[plane],
                send_sem=tsend_sem,
                recv_sem=trecv_sem,
                device_id=(there, mine),
                device_id_type=MESH,
            ).start()
        all_of(totals, zs - 1, trecv_sem).wait()

    @pl.when(core == 0)
    def _():
        all_of(totals, zs, trecv_sem).wait()

    loads[7].wait()
    all_of(gsend, n - 1, gsend_sem).wait()
    all_of(usend, n - 1, usend_sem).wait()

    all_of(parts, len(sheet) - 1, psend_sem).wait()

    @pl.when(core == 1)
    def _():
        all_of(parts, len(pillar), tsend_sem).wait()

    @pl.when(core == 0)
    def _():
        all_of(parts, 1, psend_sem).wait()

    all_of(ubuf, n - 1, urecv_sem).wait()


def store_kernel(dims, *refs):
    mats, block_rows, block_cols, width = dims
    stripe = mats * block_rows * SLAB
    done, (ubuf, onehot_t, weights, totals), rest = refs[:6], refs[6:10], refs[10:]
    step_hbm, outs, (step, sems) = rest[0], rest[1:7], rest[7:]
    copies = [pltpu.make_async_copy(a, b, sems.at[i]) for i, (a, b) in enumerate(zip(done, outs))]
    for copy in copies:
        copy.start()
    n = ubuf.shape[0]
    total = jnp.sum(totals[...])
    scale = jnp.minimum(1.0, clip_rms / jnp.sqrt(total / float(MATS * D * QW) + 1e-12))
    returned = ubuf[...].reshape(n * SLAB, width)
    for c in range(block_cols):
        placed = mm(onehot_t[c * stripe : (c + 1) * stripe, :], returned)
        at = slice(c * width, (c + 1) * width)
        step[:, at] = (scale * placed + decay_weight * weights[:, at].astype(F32)).astype(BF16)
    last = pltpu.make_async_copy(step, step_hbm, sems.at[6])
    last.start()
    for copy in copies:
        copy.wait()
    last.wait()


def body(n, groups, grads, weights, slot_block, first, second, left, right, lbasis, rbasis):
    mats, rows, cols = grads.shape
    side, width = first.shape[-2:]
    block_rows = rows // SLAB
    block_cols = cols // width
    dims = (mats, block_rows, block_cols, width)
    vmem = pltpu.VMEM
    xs = 4 if n >= 8 else 1
    zs = n // (2 * xs)
    dma = pltpu.SemaphoreType.DMA
    flat = (mats * rows, cols)
    shape = jax.ShapeDtypeStruct
    owned = [
        shape((side, width), F32),
        shape((side, width), F32),
        shape((side, side), F32),
        shape((width, width), F32),
        shape((side, side), BF16),
        shape((width, width), BF16),
    ]
    passed = [
        shape((n, SLAB, width), BF16),
        shape((side, side), BF16),
        shape(flat, BF16),
        shape((zs, 1, 128), F32),
    ]
    here = pl.BlockSpec(memory_space=pltpu.VMEM)
    away = pl.BlockSpec(memory_space=pltpu.HBM)
    results = pl.pallas_call(
        functools.partial(exchange_kernel, n, groups, dims),
        out_shape=owned + passed,
        in_specs=[away] * 9,
        out_specs=[here] * 10,
        scratch_shapes=[
            pltpu.SMEM((n,), jnp.int32),
            vmem((n, SLAB, width), BF16),
            vmem((side, width), F32),
            vmem((side, width), F32),
            vmem((side, side), F32),
            vmem((width, width), F32),
            vmem((n, SLAB, side), BF16),
            vmem((width, width), BF16),
            vmem((n, SLAB, side), F32),
            vmem((side, side), BF16),
            vmem((n, SLAB, width), BF16),
            vmem((n, SLAB, width), BF16),
            vmem((n, SLAB, width), BF16),
            vmem((2 * groups * xs, 1, 128), F32),
            pltpu.SemaphoreType.REGULAR,
            dma((8,)),
            dma((block_cols,)),
            dma,
            dma,
            dma,
            dma,
            dma,
            dma,
            dma,
            dma,
        ],
        compiler_params=pltpu.CompilerParams(
            collective_id=0, has_side_effects=True, vmem_limit_bytes=40 * 1024 * 1024
        ),
    )(
        *[
            pltpu.with_memory_space_constraint(x, pltpu.HBM)
            for x in (
                slot_block,
                grads.reshape(mats * block_rows, SLAB, cols),
                weights.reshape(flat),
                first[0, 0],
                second[0, 0],
                left[0, 0],
                right[0, 0],
                lbasis[0, 0].reshape(n, SLAB, side),
                rbasis[0, 0],
            )
        ]
    )
    stored = pl.pallas_call(
        functools.partial(store_kernel, dims),
        out_shape=[shape(flat, BF16)] + owned,
        in_specs=[here] * 10,
        out_specs=[away] * 7,
        scratch_shapes=[vmem(flat, BF16), dma((7,))],
        compiler_params=pltpu.CompilerParams(vmem_limit_bytes=40 * 1024 * 1024),
    )(*results)
    return (stored[0].reshape(grads.shape), *[r[None, None] for r in stored[1:]])


def solution(mesh):
    owned = P("mp", "dp", None, None)
    rows = P(None, "dp", "mp")
    return jax.shard_map(
        functools.partial(body, mesh.shape["dp"], mesh.shape["mp"]),
        mesh=mesh,
        in_specs=(rows, rows, P()) + (owned,) * 6,
        out_specs=(rows,) + (owned,) * 6,
        check_vma=False,
    )
```
